32 devices in a mesh: group: 2 (over x), band: 16 (over z, y, core).
Axes of the slice: x: 2, y: 2, z: 4, core: 2. Of those that a mesh axis runs over, the one named last changes fastest.
Arguments:
- grid_lat: bfloat16 [65536, 512], P(('group', 'band')), parts along dimension 0, may hold values from -6 to 6
- mesh_lat: bfloat16 [4096, 512], P(('group', 'band')), parts along dimension 0, may hold values from -6 to 6
- edge_lat: bfloat16 [4096, 16, 512], P(('group', 'band')), parts along dimension 0, may hold values from -6 to 6
- edge_w1: bfloat16 [1536, 512], replicated, may hold values from -0.15625 to 0.15625
- edge_w2: bfloat16 [512, 512], replicated, may hold values from -0.25 to 0.25
- node_w1: bfloat16 [1024, 512], replicated, may hold values from -0.1875 to 0.1875
- node_w2: bfloat16 [512, 512], replicated, may hold values from -0.25 to 0.25
- mesh_cot: bfloat16 [4096, 512], P(('group', 'band')), parts along dimension 0, may hold values from -6 to 6
- send_rows: int32 [16, 16, 64], P('band'), may hold values from 0 to 2047
- edge_src: int32 [2048, 16], P('band'), may hold values from 0 to 1023, as said below
- edge_mask: int32 [2048, 16], P('band'), may hold values 0 or 1
Outputs:
- mesh_new: bfloat16 [4096, 512], P(('group', 'band')), parts along dimension 0
- grid_grad: bfloat16 [65536, 512], P(('group', 'band')), parts along dimension 0
- w1_grad: float32 [3072, 512], P(('group', 'band')), parts along dimension 0
The draws below stay inside these ranges and needn't reach their ends.
There are 2 independent parts, one for each index of `group`. The reference program is written for one: setup_inputs(seed, part) draws one part's arguments, and reference() takes and returns one part's arrays. A program takes and returns all parts, laid end to end along the dimension named above; an argument that names none is the same for every part. Nothing has to cross between parts.
Inputs may be any that keep to these rules, and one draw needn't show every extreme that they name: edge_src[i, k] = j * 64 + c names slot c of the rows that device (d - j + 8) mod 16 sends to the device d of mesh node i; c stays below a count of 1 to 64 of that pair, and each device receives 64 live slots from at least one sender.
All inputs are finite; a program needn't handle non-finite values. No bound on the sum of `edge_mask` on one device may be relied on, other than what follows from the above.
Results may differ from the reference program's by a relative error of at most 0.014.
Values may be sent and summed in bfloat16 or wider, within the bound.
No kernel may reach another device: no remote copies, remote signals or barrier semaphores. Data moves between devices by JAX's collectives and lax.ppermute only.
A program may use at most 128 MiB of HBM per device.

```python
import jax
import jax.numpy as jnp
from jax import lax

W = 512
K = 16
WIN = 16
MESH_DEV = 128
GRID_DEV = 2048
CAP = 64
MESH = 2048
GRID = 32768
N_BAND = 16


def draw_edge_src(key, part):
    key = jax.random.fold_in(key, 7)
    key_count, key_peer, key_slot = jax.random.split(key, 3)
    devices = N_BAND
    low = max(1, (CAP + 2) // 3)
    counts = jax.random.randint(key_count, (devices, WIN), low, CAP + 1)
    cols = jnp.arange(WIN, dtype=jnp.int32)[None, :]
    full_slot = WIN // 2 + 1
    counts = jnp.where(cols == full_slot, CAP, counts)
    window_slot = jax.random.randint(key_peer, (devices, MESH_DEV * K), 0, WIN)
    raw_slot = jax.random.randint(key_slot, (devices, MESH_DEV * K), 0, 65520)
    chosen = jnp.take_along_axis(counts, window_slot, axis=1)
    index = window_slot * CAP + raw_slot % chosen
    index = index.at[:, 0].set(full_slot * CAP + CAP - 1)
    index = index.at[:, 1].set(full_slot * CAP)
    return index.reshape(devices * MESH_DEV, K).astype(jnp.int32)


def set_ends(array, own_key, low, top_value):
    dims = array.shape
    index_at = [jax.random.randint(jax.random.fold_in(own_key, axis), (), 0, dims[axis]) for axis in range(len(dims))]
    array = array.at[tuple(index_at)].set(low)
    longest = dims.index(max(dims))
    index_at[longest] = (index_at[longest] + 1) % dims[longest]
    return array.at[tuple(index_at)].set(top_value)


def raised(result, own_key, source, target, parts, factor):
    def block_of(dim):
        return (jnp.arange(result.shape[dim]) // (result.shape[dim] // parts)).reshape((-1,) + (1,) * (result.ndim - 1 - dim))

    near = jax.random.permutation(own_key, parts)[block_of(target)]
    second = (block_of(target) + parts // 2) % parts
    return jnp.where((block_of(source) == near) | (block_of(source) == second), factor * result, result)


def steps_of(own_key, shape, cuts, least, top_value):
    loudness, own = 1.0, jax.random.fold_in(own_key, 6)
    for position, shards_of in cuts:
        steps = jnp.exp(jax.random.uniform(jax.random.fold_in(own, position), (shards_of,), jnp.float32, least / len(cuts), top_value / len(cuts)))
        loudness = loudness * jnp.repeat(steps, shape[position] // shards_of).reshape([-1 if axis == position else 1 for axis in range(len(shape))])
    return loudness


def normal_values(own_key, dims, spread, limit, shards=(), kind=jnp.bfloat16):
    level = steps_of(own_key, dims, shards, -0.22, 0.18) if shards else 1.0
    result = jax.random.normal(own_key, dims, jnp.float32) * spread * level
    return jnp.minimum(jnp.maximum(result, -limit), limit).astype(kind)


def bell_draw_with(key, extent, deviation, reach, shards, heavy, kind=jnp.bfloat16):
    array = deviation * jax.random.normal(key, extent, jnp.float32)
    if shards:
        array = array * steps_of(key, extent, shards, -0.22, 0.18)
    return jnp.clip(raised(array, jax.random.fold_in(key, 3), *heavy), -reach, reach).astype(kind)


def setup_inputs(seed: int = 0, part: int = 0) -> dict:
    arg_keys = jax.random.split(jax.random.key(seed), 12)
    part_keys = jax.random.split(jax.random.fold_in(arg_keys[11], part), 12)
    grid_lat = normal_values(part_keys[0], (GRID, W), 1.0, 6.0, ((0, 16),))
    mesh_lat = normal_values(part_keys[1], (MESH, W), 1.0, 6.0, ((0, 16),))
    edge_lat = bell_draw_with(part_keys[2], (MESH, K, W), 1.0, 6.0, ((0, 16),), (0, 2, 16, 2.0))
    edge_w1 = normal_values(arg_keys[3], (3 * W, W), (3 * W) ** -0.5, 0.15625)
    edge_w2 = normal_values(arg_keys[4], (W, W), W ** -0.5, 0.25)
    node_w1 = normal_values(arg_keys[5], (2 * W, W), (2 * W) ** -0.5, 0.1875)
    node_w2 = normal_values(arg_keys[6], (W, W), W ** -0.5, 0.25)
    mesh_cot = normal_values(part_keys[7], (MESH, W), 1.0, 6.0, ((0, 16),))
    send_rows = set_ends(jax.random.randint(arg_keys[8], (N_BAND, WIN, CAP), 0, GRID_DEV), jax.random.fold_in(arg_keys[8], 1), 0, GRID_DEV - 1).astype(jnp.int32)
    edge_src = draw_edge_src(jax.random.fold_in(arg_keys[11], 71), part)
    edge_mask = set_ends((jax.random.randint(arg_keys[10], (MESH, K), 0, 5) < 4).astype(jnp.int32), jax.random.fold_in(arg_keys[10], 1), 0, 1)
    return dict(grid_lat=grid_lat, mesh_lat=mesh_lat, edge_lat=edge_lat, edge_w1=edge_w1, edge_w2=edge_w2, node_w1=node_w1, node_w2=node_w2, mesh_cot=mesh_cot, send_rows=send_rows, edge_src=edge_src, edge_mask=edge_mask)


eps = 1e-05

def layer_norm(value):
    centred = value - lax.optimization_barrier(jnp.mean(value, axis=-1, keepdims=True))
    scale = lax.rsqrt(lax.optimization_barrier(jnp.mean(centred * centred, axis=-1, keepdims=True)) + eps)
    return centred * scale

def norm_back(value, grad):
    centred = value - lax.optimization_barrier(jnp.mean(value, axis=-1, keepdims=True))
    scale = lax.rsqrt(lax.optimization_barrier(jnp.mean(centred * centred, axis=-1, keepdims=True)) + eps)
    normed = centred * scale
    return scale * (grad - lax.optimization_barrier(jnp.mean(grad, axis=-1, keepdims=True)) - normed * lax.optimization_barrier(jnp.mean(grad * normed, axis=-1, keepdims=True)))

def silu_grad(value):
    sig = jax.nn.sigmoid(value)
    return sig * (1.0 + value * (1.0 - sig))

def reference(grid_lat, mesh_lat, edge_lat, edge_w1, edge_w2, node_w1, node_w2, mesh_cot, send_rows, edge_src, edge_mask):
    width = W
    w1e = edge_w1[:width]
    w1g = edge_w1[width:2 * width]
    w1m = edge_w1[2 * width:]
    v1m = node_w1[:width]
    v1a = node_w1[width:]
    f32 = jnp.float32
    bf16 = jnp.bfloat16
    window_ids = jnp.arange(WIN, dtype=jnp.int32)

    def block(carry, inputs):
        grid_acc, term_acc = carry
        dev, mesh_blk, edge_blk, cot_blk, src_blk, mask_blk = inputs
        senders = ((dev - window_ids + WIN // 2) % N_BAND).astype(jnp.int32)
        table = send_rows[senders, window_ids]
        global_ids = (senders[:, None] * GRID_DEV + table).reshape(-1).astype(jnp.int32)
        arrived = grid_lat[global_ids]
        proj = jnp.dot(arrived, w1g, preferred_element_type=f32).astype(bf16)
        flat_src = src_blk.reshape(-1)
        edges = edge_blk.reshape(-1, width)
        mesh_rep = jnp.repeat(mesh_blk, K, axis=0)
        maskf = mask_blk.reshape(-1, 1).astype(f32)
        pre1 = jnp.dot(edges, w1e, preferred_element_type=f32) + jnp.dot(mesh_rep, w1m, preferred_element_type=f32) + proj[flat_src].astype(f32)
        hid = jax.nn.silu(pre1).astype(bf16)
        pre2 = jnp.dot(hid, edge_w2, preferred_element_type=f32)
        msg = layer_norm(pre2) * maskf
        agg = lax.optimization_barrier(jnp.sum(msg.reshape(MESH_DEV, K, width), axis=1)).astype(bf16)
        pre3 = jnp.dot(mesh_blk, v1m, preferred_element_type=f32) + jnp.dot(agg, v1a, preferred_element_type=f32)
        act = jax.nn.silu(pre3).astype(bf16)
        pre4 = jnp.dot(act, node_w2, preferred_element_type=f32)
        new_blk = (mesh_blk.astype(f32) + layer_norm(pre4)).astype(bf16)
        g4 = norm_back(pre4, cot_blk.astype(f32)).astype(bf16)
        g3 = (jnp.dot(g4, node_w2.T, preferred_element_type=f32) * silu_grad(pre3)).astype(bf16)
        gagg = jnp.dot(g3, v1a.T, preferred_element_type=f32)
        g2 = norm_back(pre2, jnp.repeat(gagg, K, axis=0) * maskf).astype(bf16)
        g1 = (jnp.dot(g2, edge_w2.T, preferred_element_type=f32) * silu_grad(pre1)).astype(bf16)
        gproj = jnp.zeros((WIN * CAP, width), f32).at[flat_src].add(g1.astype(f32)).astype(bf16)
        gslot = jnp.dot(gproj, w1g.T, preferred_element_type=f32)
        term_e = jnp.einsum('ew,ev->wv', edges.astype(f32), g1.astype(f32))
        term_g = jnp.einsum('ew,ev->wv', arrived.astype(f32), gproj.astype(f32))
        term_m = jnp.einsum('ew,ev->wv', mesh_rep.astype(f32), g1.astype(f32))
        term = jnp.concatenate([term_e, term_g, term_m], axis=0)
        grid_acc = grid_acc.at[global_ids].add(gslot)
        return ((grid_acc, term_acc + term), new_blk)
    init = (jnp.zeros((GRID, width), f32), jnp.zeros((3 * width, width), f32))
    xs = (jnp.arange(N_BAND, dtype=jnp.int32), mesh_lat.reshape(N_BAND, MESH_DEV, width), edge_lat.reshape(N_BAND, MESH_DEV, K, width), mesh_cot.reshape(N_BAND, MESH_DEV, width), edge_src.reshape(N_BAND, MESH_DEV, K), edge_mask.reshape(N_BAND, MESH_DEV, K))
    (grid_acc, term_acc), new_blocks = lax.scan(block, init, xs)
    return (new_blocks.reshape(MESH, width), grid_acc.astype(bf16), term_acc)
```

```python
import functools

import jax
import jax.numpy as jnp
from jax import lax
from jax.experimental import pallas as pl
from jax.experimental.pallas import tpu as pltpu
from jax.sharding import PartitionSpec as P

eps = 1e-05
f32 = jnp.float32
bf16 = jnp.bfloat16
ANY = pl.BlockSpec(memory_space=pl.ANY)
VM = pl.BlockSpec(memory_space=pltpu.VMEM)


def from_behind(array, axis, by):
    devices = lax.axis_size(axis)
    return lax.ppermute(array, axis, [(i, (i + by) % devices) for i in range(devices)])


def layer_norm(value):
    centred = value - jnp.mean(value, axis=-1, keepdims=True)
    scale = lax.rsqrt(jnp.mean(centred * centred, axis=-1, keepdims=True) + eps)
    return centred * scale


def norm_back(value, grad):
    centred = value - jnp.mean(value, axis=-1, keepdims=True)
    scale = lax.rsqrt(jnp.mean(centred * centred, axis=-1, keepdims=True) + eps)
    normed = centred * scale
    return scale * (
        grad
        - jnp.mean(grad, axis=-1, keepdims=True)
        - normed * jnp.mean(grad * normed, axis=-1, keepdims=True)
    )


def silu_grad(value):
    sig = jax.nn.sigmoid(value)
    return sig * (1.0 + value * (1.0 - sig))


def outer_sum(left, right):
    return lax.dot_general(
        left, right, (((0,), (0,)), ((), ())), preferred_element_type=f32
    )


def mm(left, right):
    return jnp.dot(left, right, preferred_element_type=f32)


def mm_t(left, right):
    return lax.dot_general(
        left, right, (((1,), (1,)), ((), ())), preferred_element_type=f32
    )


def send_forward(outgoing):
    window = outgoing.shape[0]
    half = window // 2
    pieces = []
    for slot in range(window):
        offset = slot - half
        if offset == 0:
            pieces.append(outgoing[slot])
        else:
            pieces.append(from_behind(outgoing[slot], "band", offset))
    return jnp.stack(pieces, axis=0)


def return_rows(grads):
    window = grads.shape[0]
    half = window // 2
    pieces = []
    for slot in range(window):
        offset = slot - half
        if offset == 0:
            pieces.append(grads[slot])
        else:
            pieces.append(
                from_behind(grads[slot].astype(bf16), "band", -offset).astype(f32)
            )
    return jnp.stack(pieces, axis=0)


def per_device_window(
    grid_lat, mesh_lat, edge_lat, edge_w1, edge_w2, node_w1, node_w2, mesh_cot,
    send_rows, edge_src, edge_mask,
):
    width = mesh_lat.shape[1]
    nodes, slots = edge_src.shape
    window = send_rows.shape[1]
    cap = send_rows.shape[2]
    w1e = edge_w1[:width]
    w1g = edge_w1[width : 2 * width]
    w1m = edge_w1[2 * width :]
    v1m = node_w1[:width]
    v1a = node_w1[width:]
    row_ids = send_rows[0].reshape(-1)
    outgoing_raw = grid_lat[row_ids]
    arrived = send_forward(outgoing_raw.reshape(window, cap, width)).reshape(window * cap, width)
    proj = mm(arrived, w1g).astype(bf16)
    flat_src = edge_src.reshape(-1)
    edges = edge_lat.reshape(nodes * slots, width)
    mesh_rep = jnp.repeat(mesh_lat, slots, axis=0)
    maskf = edge_mask.reshape(-1, 1).astype(f32)
    pre1 = mm(edges, w1e) + mm(mesh_rep, w1m) + proj[flat_src].astype(f32)
    hid = jax.nn.silu(pre1).astype(bf16)
    pre2 = mm(hid, edge_w2)
    msg = layer_norm(pre2) * maskf
    agg = jnp.sum(msg.reshape(nodes, slots, width), axis=1).astype(bf16)
    pre3 = mm(mesh_lat, v1m) + mm(agg, v1a)
    act = jax.nn.silu(pre3).astype(bf16)
    pre4 = mm(act, node_w2)
    mesh_new = (mesh_lat.astype(f32) + layer_norm(pre4)).astype(bf16)
    g4 = norm_back(pre4, mesh_cot.astype(f32)).astype(bf16)
    g3 = (mm(g4, node_w2.T) * silu_grad(pre3)).astype(bf16)
    gagg = mm(g3, v1a.T)
    g2 = norm_back(pre2, jnp.repeat(gagg, slots, axis=0) * maskf).astype(bf16)
    g1 = (mm(g2, edge_w2.T) * silu_grad(pre1)).astype(bf16)
    gproj = jnp.zeros((window * cap, width), f32).at[flat_src].add(g1.astype(f32)).astype(bf16)
    term_e = outer_sum(edges, g1)
    term_m = outer_sum(mesh_rep, g1)
    term_g = outer_sum(arrived, gproj)
    local_slot = mm(gproj, w1g.T)
    gslot = return_rows(local_slot.reshape(window, cap, width)).reshape(window * cap, width)
    grid_grad = jnp.zeros((grid_lat.shape[0], width), f32).at[row_ids].add(gslot).astype(bf16)
    term = jnp.concatenate([term_e, term_g, term_m], axis=0)
    w1_grad = lax.psum_scatter(term, "band", scatter_dimension=0, tiled=True)
    return (mesh_new, grid_grad, w1_grad)


SEND_A = [4 * kz + 2 * ky for ky in range(2) for kz in range(4)]
SEND_B = [4 * kz + 2 * ky + 1 for kz in range(4) for ky in range(2)]
RECV_A = [4 * kz + 2 * ky for kz in range(4) for ky in range(2)]
RECV_B = [4 * kz + 2 * ky + 1 for ky in range(2) for kz in range(4)]
SEND = SEND_A + SEND_B
RECV = RECV_A + RECV_B


def places(order):
    out = [0] * len(order)
    for place, k in enumerate(order):
        out[k] = place
    return out


def swap(array, k):
    return lax.ppermute(array, "band", [(i, i ^ k) for i in range(16)])


def exchange(a0, a1, b):
    half = b[0].shape[0] // 2
    bz = [b[0]] + [None] * 3
    for kz in (2, 3, 1):
        bz[kz] = swap(b[kz], 4 * kz)
    ay = swap(a1, 2)
    az = [None] * 4
    for kz in (0, 2, 3, 1):
        piece = jnp.concatenate(
            [a0[kz * half : (kz + 1) * half], ay[kz * half : (kz + 1) * half]], axis=0
        )
        az[kz] = swap(piece, 4 * kz) if kz else piece
    by = swap(jnp.concatenate([piece[half:] for piece in bz], axis=0), 2)
    bc = swap(jnp.concatenate([piece[:half] for piece in bz] + [by], axis=0), 1)
    return az, bc


def gather_kernel(order, ids_ref, grid_ref, *rest):
    outs, sel = rest[:-1], rest[-1]
    cap = ids_ref.shape[2]
    grid_rows = grid_ref.shape[0]
    d = lax.axis_index("band")
    table = jnp.transpose(ids_ref[0].astype(f32))
    lane = lax.broadcasted_iota(jnp.int32, table.shape, 1)
    column = lax.broadcasted_iota(jnp.int32, (cap, grid_rows), 1)
    per = outs[0].shape[0] // cap
    for place, k in enumerate(order):
        j = ((d ^ k) - d + 8) & 15
        ids = jnp.sum(jnp.where(lane == j, table, 0.0), axis=1, keepdims=True).astype(jnp.int32)
        at = place % per
        sel[at * cap : (at + 1) * cap] = (ids == column).astype(f32).astype(bf16)
        if at == per - 1:
            outs[place // per][...] = mm(sel[...], grid_ref[...]).astype(bf16)


def gather(order, pieces, send_rows, grid_lat):
    cap = send_rows.shape[2]
    rows = len(order) * cap // pieces
    shape = jax.ShapeDtypeStruct((rows, grid_lat.shape[1]), bf16)
    return pl.pallas_call(
        functools.partial(gather_kernel, order),
        out_shape=[shape] * pieces,
        in_specs=[VM, VM],
        out_specs=[VM] * pieces,
        scratch_shapes=[pltpu.VMEM((rows, grid_lat.shape[0]), bf16)],
        compiler_params=pltpu.CompilerParams(vmem_limit_bytes=32 << 20),
        cost_estimate=pl.CostEstimate(
            flops=2 * rows * pieces * grid_lat.size, bytes_accessed=3 << 20, transcendentals=0
        ),
        name="gather_rows",
    )(send_rows, grid_lat)


def sigmoid(v):
    return 1.0 / (1.0 + jnp.exp(-v))


def row_mean(v):
    return jnp.mean(v, axis=-1, keepdims=True)


STEP = 256


def middle_kernel(
    pre_ref, hot_ref, az0, az1, az2, az3, bc, w1g_ref, w2_ref, mesh_ref, cot_ref, v1_ref, n2_ref,
    mask_ref, src_ref,
    new_ref, g1_ref, gb_ref, s0, s1, s2, s3,
    arrived, proj, pre, hot, hn, rm, agg, gagg, sems,
):
    width = w2_ref.shape[0]
    nodes = mesh_ref.shape[0]
    total = pre_ref.shape[0]
    steps = total // STEP
    loads = []
    at = 0
    for i, piece in enumerate((az0, az1, az2, az3, bc)):
        rows = piece.shape[0]
        loads.append(pltpu.make_async_copy(piece, arrived.at[at : at + rows], sems.at[i]))
        at += rows
    for i in range(steps):
        part = slice(i * STEP, (i + 1) * STEP)
        loads.append(pltpu.make_async_copy(pre_ref.at[part], pre.at[part], sems.at[5 + 2 * i]))
        loads.append(pltpu.make_async_copy(hot_ref.at[part], hot.at[part], sems.at[6 + 2 * i]))
    for copy in loads:
        copy.start()
    for copy in loads[:5]:
        copy.wait()
    proj[...] = mm(arrived[...], w1g_ref[...]).astype(bf16)
    agg[...] = jnp.zeros_like(agg)
    for i in range(steps):
        part = slice(i * STEP, (i + 1) * STEP)
        loads[5 + 2 * i].wait()
        loads[6 + 2 * i].wait()
        v = pre[part] + mm(hot[part], proj[...])
        sig = sigmoid(v)
        hid = v * sig
        pre[part] = sig + hid * (1.0 - sig)
        p2 = mm(hid.astype(bf16), w2_ref[...])
        c = p2 - row_mean(p2)
        r = lax.rsqrt(row_mean(c * c) + eps)
        h = c * r
        hn[part] = h
        m = mask_ref[part]
        rm[part] = r * m
        msg = h * m
        add = msg[:nodes]
        for n in range(1, STEP // nodes):
            add = add + msg[n * nodes : (n + 1) * nodes]
        agg[...] += add
    mesh = mesh_ref[...]
    p3 = mm(mesh, v1_ref[:width]) + mm(agg[...].astype(bf16), v1_ref[width:])
    sig = sigmoid(p3)
    a3 = p3 * sig
    p4 = mm(a3.astype(bf16), n2_ref[...])
    c = p4 - row_mean(p4)
    r = lax.rsqrt(row_mean(c * c) + eps)
    h = c * r
    new_ref[...] = (mesh.astype(f32) + h).astype(bf16)
    cot = cot_ref[...].astype(f32)
    g4 = (r * (cot - row_mean(cot) - h * row_mean(cot * h))).astype(bf16)
    g3 = (mm_t(g4, n2_ref[...]) * (sig + a3 * (1.0 - sig))).astype(bf16)
    ga = mm_t(g3, v1_ref[width:])
    gagg[...] = ga
    for i in range(steps):
        part = slice(i * STEP, (i + 1) * STEP)
        ga = jnp.concatenate([gagg[...]] * (STEP // nodes), axis=0)
        h = hn[part]
        g2 = rm[part] * (ga - row_mean(ga) - h * row_mean(ga * h))
        g1_ref[part] = (mm_t(g2.astype(bf16), w2_ref[...]) * pre[part]).astype(bf16)
    scatter_slots(g1_ref, src_ref, w1g_ref, bc.shape[0], gb_ref, (s0, s1, s2, s3))


def scatter_slots(g1_ref, src_ref, w1g_ref, first, gp_ref, outs):
    rows = outs[0].shape[0]
    src = src_ref[...]
    for i, out in enumerate(outs):
        slot = lax.broadcasted_iota(jnp.int32, (rows, src.shape[1]), 0) + (first + i * rows)
        sel = (slot == src).astype(f32).astype(bf16)
        gp = mm(sel, g1_ref[...]).astype(bf16)
        gp_ref[i * rows : (i + 1) * rows] = gp
        out[...] = mm_t(gp, w1g_ref[...]).astype(bf16)


def middle(pre, hot, az, bc, w1g, w2, mesh_lat, cot, v1, n2, mask, src):
    total, width = pre.shape
    slots = hot.shape[1]
    nodes = mesh_lat.shape[0]
    sd = jax.ShapeDtypeStruct
    half = slots // 2
    return pl.pallas_call(
        middle_kernel,
        out_shape=[
            sd((nodes, width), bf16), sd((total, width), bf16), sd((half, width), bf16),
        ] + [sd((half // 4, width), bf16)] * 4,
        in_specs=[ANY] * 7 + [VM] * 8,
        out_specs=[VM] * 7,
        scratch_shapes=[
            pltpu.VMEM((slots, width), bf16),
            pltpu.VMEM((slots, width), bf16),
            pltpu.VMEM((total, width), f32),
            pltpu.VMEM((total, slots), bf16),
            pltpu.VMEM((total, width), f32),
            pltpu.VMEM((total, 1), f32),
            pltpu.VMEM((nodes, width), f32),
            pltpu.VMEM((nodes, width), f32),
            pltpu.SemaphoreType.DMA((5 + 2 * (total // STEP),)),
        ],
        compiler_params=pltpu.CompilerParams(vmem_limit_bytes=40 << 20),
        cost_estimate=pl.CostEstimate(
            flops=12 * total * width * width, bytes_accessed=16 << 20, transcendentals=2 * total * width
        ),
        name="edges_and_nodes",
    )(pre, hot, *az, bc, w1g, w2, mesh_lat, cot, v1, n2, mask, src)


def slots_a_kernel(g1_ref, src_ref, w1g_ref, ga_ref, s0, s1):
    scatter_slots(g1_ref, src_ref, w1g_ref, 0, ga_ref, (s0, s1))


def slots_a(g1, src, w1g, half):
    width = g1.shape[1]
    sd = jax.ShapeDtypeStruct
    return pl.pallas_call(
        slots_a_kernel,
        out_shape=[sd((half, width), bf16)] + [sd((half // 2, width), bf16)] * 2,
        in_specs=[VM] * 3,
        out_specs=[VM] * 3,
        compiler_params=pltpu.CompilerParams(vmem_limit_bytes=32 << 20),
        cost_estimate=pl.CostEstimate(
            flops=2 * half * width * g1.shape[0], bytes_accessed=4 << 20, transcendentals=0
        ),
        name="slots_a",
    )(g1, src, w1g)


SHARE = [4 * kz + 2 * ky for ky in range(2) for kz in (0, 2, 1, 3)]


def terms_kernel(et_ref, g1_ref, mesh_ref, at_ref, gp_ref, keep_ref, send_ref, term):
    width = g1_ref.shape[1]
    nodes = mesh_ref.shape[0]
    total = g1_ref.shape[0]
    share = keep_ref.shape[1]
    d = lax.axis_index("band")
    g1 = g1_ref[...]
    term[:width] = mm(et_ref[...], g1)
    term[width : 2 * width] = mm(at_ref[...], gp_ref[...])
    gsum = g1[:nodes].astype(f32)
    for k in range(1, total // nodes):
        gsum = gsum + g1[k * nodes : (k + 1) * nodes].astype(f32)
    term[2 * width :] = outer_sum(mesh_ref[...], gsum.astype(bf16))
    for i, k in enumerate(SHARE):
        keep_ref[i] = term[pl.ds(pl.multiple_of((d ^ k) * share, share), share)]
        send_ref[i] = term[pl.ds(pl.multiple_of((d ^ k ^ 1) * share, share), share)].astype(bf16)


def terms(edges_t, g1, mesh_lat, arrived_t, gproj):
    width = g1.shape[1]
    share = 3 * width // 16
    sd = jax.ShapeDtypeStruct
    return pl.pallas_call(
        terms_kernel,
        out_shape=[sd((8, share, width), f32), sd((8, share, width), bf16)],
        in_specs=[VM] * 5,
        out_specs=[VM] * 2,
        scratch_shapes=[pltpu.VMEM((3 * width, width), f32)],
        compiler_params=pltpu.CompilerParams(vmem_limit_bytes=40 << 20),
        cost_estimate=pl.CostEstimate(
            flops=4 * width * width * g1.shape[0], bytes_accessed=8 << 20, transcendentals=0
        ),
        name="w1_terms",
    )(edges_t, g1, mesh_lat, arrived_t, gproj)


def share_sum(keep, send):
    for k in (1, 2, 4, 8):
        full = keep + swap(send, k).astype(f32)
        half = full.shape[0] // 2
        if half:
            keep, send = full[:half], full[half:].astype(bf16)
    return full[0]


def grid_kernel(ids_ref, a0, a1, a2, a3, bc, out_ref, rows_ref):
    at = 0
    for piece in (a0, a1, a2, a3, bc):
        rows_ref[at : at + piece.shape[0]] = piece[...]
        at += piece.shape[0]
    ids = ids_ref[...]
    block = 256
    for i in range(out_ref.shape[0] // block):
        row = lax.broadcasted_iota(jnp.int32, (block, ids.shape[1]), 0) + i * block
        sel = (row == ids).astype(f32).astype(bf16)
        out_ref[i * block : (i + 1) * block] = mm(sel, rows_ref[...]).astype(bf16)


def grid_sum(ids, az, bc, grid_rows):
    width = bc.shape[1]
    return pl.pallas_call(
        grid_kernel,
        out_shape=jax.ShapeDtypeStruct((grid_rows, width), bf16),
        in_specs=[VM] * 6,
        out_specs=VM,
        scratch_shapes=[pltpu.VMEM((ids.shape[1], width), bf16)],
        compiler_params=pltpu.CompilerParams(vmem_limit_bytes=32 << 20),
        cost_estimate=pl.CostEstimate(
            flops=2 * grid_rows * ids.shape[1] * width, bytes_accessed=4 << 20, transcendentals=0
        ),
        name="grid_sum",
    )(ids, *az, bc)


def per_device_all(
    grid_lat, mesh_lat, edge_lat, edge_w1, edge_w2, node_w1, node_w2, mesh_cot,
    send_rows, edge_src, edge_mask,
):
    width = mesh_lat.shape[1]
    nodes, slots = edge_src.shape
    window, cap = send_rows.shape[1:]
    total = nodes * slots
    half = window * cap // 2
    d = lax.axis_index("band")
    w1e = edge_w1[:width]
    w1g = edge_w1[width : 2 * width]
    w1m = edge_w1[2 * width :]

    b = gather(SEND_B, 4, send_rows, grid_lat)
    a0, a1 = gather(SEND_A, 2, send_rows, grid_lat)
    az, bc = exchange(a0, a1, b)

    edges = jnp.transpose(edge_lat, (1, 0, 2)).reshape(total, width)
    own = mm(edges, w1e).reshape(slots, nodes, width) + mm(mesh_lat, w1m)[None]
    pre = own.reshape(total, width)
    src = jnp.transpose(edge_src).reshape(total)
    peer = d ^ ((d - src // cap + 8) & 15)
    recv_at = jnp.asarray(places(RECV), jnp.int32)
    send_at = jnp.asarray(places(SEND), jnp.int32)
    ks = jnp.arange(16, dtype=jnp.int32)
    pick = (peer[:, None] == ks[None, :]).astype(jnp.int32)
    src_recv = jnp.sum(pick * recv_at[None, :], axis=1) * cap + src % cap
    src_send = jnp.sum(pick * send_at[None, :], axis=1) * cap + src % cap
    hot = (src_recv[:, None] == jnp.arange(window * cap, dtype=jnp.int32)[None, :]).astype(bf16)
    mask = jnp.transpose(edge_mask).reshape(total, 1).astype(f32)
    src_row = src_send.reshape(1, total)
    edges_t = jnp.transpose(edges)

    out = middle(
        pre, hot, az, bc, w1g, edge_w2, mesh_lat, mesh_cot, node_w1, node_w2, mask, src_row
    )
    mesh_new, g1, gp_b = out[:3]
    gp_a, ra0, ra1 = slots_a(g1, src_row, w1g, half)
    raz, rbc = exchange(ra0, ra1, out[3:])

    blocks = [None] * window
    for kz in range(4):
        for ky in range(2):
            blocks[4 * kz + 2 * ky] = az[kz][ky * cap : (ky + 1) * cap]
            at = (ky * 4 + kz) * cap
            blocks[4 * kz + 2 * ky + 1] = bc[at : at + cap]
    arrived_t = jnp.transpose(jnp.concatenate([blocks[k] for k in SEND], axis=0))
    gproj = jnp.concatenate([gp_a, gp_b], axis=0)
    keep, send = terms(edges_t, g1, mesh_lat, arrived_t, gproj)
    w1_grad = share_sum(keep, send)

    j = ((d ^ jnp.asarray(RECV, jnp.int32)) - d + 8) & 15
    ids = send_rows[0][j].reshape(1, window * cap)
    grid_grad = grid_sum(ids, raz, rbc, grid_lat.shape[0])
    return (mesh_new, grid_grad, w1_grad)


def solution(mesh):
    in_specs = (
        P(("group", "band"), None),
        P(("group", "band"), None),
        P(("group", "band"), None, None),
        P(),
        P(),
        P(),
        P(),
        P(("group", "band"), None),
        P("band", None, None),
        P("band", None),
        P("band", None),
    )
    out_specs = (P(("group", "band"), None), P(("group", "band"), None), P(("group", "band"), None))

    def step(*args):
        window = args[8].shape[1]
        every = mesh.shape["band"] == window == 16
        body = per_device_all if every else per_device_window
        return jax.shard_map(
            body, mesh=mesh, in_specs=in_specs, out_specs=out_specs, check_vma=False
        )(*args)

    return step
```

```python
import functools

import jax
import jax.numpy as jnp
from jax import lax
from jax.experimental import pallas as pl
from jax.experimental.pallas import tpu as pltpu
from jax.sharding import PartitionSpec as P

eps = 1e-05
f32 = jnp.float32
bf16 = jnp.bfloat16
VM = pl.BlockSpec(memory_space=pltpu.VMEM)
HBM = pl.BlockSpec(memory_space=pltpu.HBM)
VMEM = 56 << 20
QUICK = pl.CostEstimate(flops=1, bytes_accessed=1, transcendentals=0)


def from_behind(array, axis, by):
    devices = lax.axis_size(axis)
    return lax.ppermute(array, axis, [(i, (i + by) % devices) for i in range(devices)])


def layer_norm(value):
    centred = value - jnp.mean(value, axis=-1, keepdims=True)
    scale = lax.rsqrt(jnp.mean(centred * centred, axis=-1, keepdims=True) + eps)
    return centred * scale


def norm_back(value, grad):
    centred = value - jnp.mean(value, axis=-1, keepdims=True)
    scale = lax.rsqrt(jnp.mean(centred * centred, axis=-1, keepdims=True) + eps)
    normed = centred * scale
    return scale * (
        grad
        - jnp.mean(grad, axis=-1, keepdims=True)
        - normed * jnp.mean(grad * normed, axis=-1, keepdims=True)
    )


def silu_grad(value):
    sig = jax.nn.sigmoid(value)
    return sig * (1.0 + value * (1.0 - sig))


def outer_sum(left, right):
    return lax.dot_general(
        left, right, (((0,), (0,)), ((), ())), preferred_element_type=f32
    )


def mm(left, right):
    return jnp.dot(left, right, preferred_element_type=f32)


def mm_t(left, right):
    return lax.dot_general(
        left, right, (((1,), (1,)), ((), ())), preferred_element_type=f32
    )


def send_forward(outgoing):
    window = outgoing.shape[0]
    half = window // 2
    pieces = []
    for slot in range(window):
        offset = slot - half
        if offset == 0:
            pieces.append(outgoing[slot])
        else:
            pieces.append(from_behind(outgoing[slot], "band", offset))
    return jnp.stack(pieces, axis=0)


def return_rows(grads):
    window = grads.shape[0]
    half = window // 2
    pieces = []
    for slot in range(window):
        offset = slot - half
        if offset == 0:
            pieces.append(grads[slot])
        else:
            pieces.append(
                from_behind(grads[slot].astype(bf16), "band", -offset).astype(f32)
            )
    return jnp.stack(pieces, axis=0)


def per_device_window(
    grid_lat, mesh_lat, edge_lat, edge_w1, edge_w2, node_w1, node_w2, mesh_cot,
    send_rows, edge_src, edge_mask,
):
    width = mesh_lat.shape[1]
    nodes, slots = edge_src.shape
    window = send_rows.shape[1]
    cap = send_rows.shape[2]
    w1e = edge_w1[:width]
    w1g = edge_w1[width : 2 * width]
    w1m = edge_w1[2 * width :]
    v1m = node_w1[:width]
    v1a = node_w1[width:]
    row_ids = send_rows[0].reshape(-1)
    outgoing_raw = grid_lat[row_ids]
    arrived = send_forward(outgoing_raw.reshape(window, cap, width)).reshape(window * cap, width)
    proj = mm(arrived, w1g).astype(bf16)
    flat_src = edge_src.reshape(-1)
    edges = edge_lat.reshape(nodes * slots, width)
    mesh_rep = jnp.repeat(mesh_lat, slots, axis=0)
    maskf = edge_mask.reshape(-1, 1).astype(f32)
    pre1 = mm(edges, w1e) + mm(mesh_rep, w1m) + proj[flat_src].astype(f32)
    hid = jax.nn.silu(pre1).astype(bf16)
    pre2 = mm(hid, edge_w2)
    msg = layer_norm(pre2) * maskf
    agg = jnp.sum(msg.reshape(nodes, slots, width), axis=1).astype(bf16)
    pre3 = mm(mesh_lat, v1m) + mm(agg, v1a)
    act = jax.nn.silu(pre3).astype(bf16)
    pre4 = mm(act, node_w2)
    mesh_new = (mesh_lat.astype(f32) + layer_norm(pre4)).astype(bf16)
    g4 = norm_back(pre4, mesh_cot.astype(f32)).astype(bf16)
    g3 = (mm(g4, node_w2.T) * silu_grad(pre3)).astype(bf16)
    gagg = mm(g3, v1a.T)
    g2 = norm_back(pre2, jnp.repeat(gagg, slots, axis=0) * maskf).astype(bf16)
    g1 = (mm(g2, edge_w2.T) * silu_grad(pre1)).astype(bf16)
    gproj = jnp.zeros((window * cap, width), f32).at[flat_src].add(g1.astype(f32)).astype(bf16)
    term_e = outer_sum(edges, g1)
    term_m = outer_sum(mesh_rep, g1)
    term_g = outer_sum(arrived, gproj)
    local_slot = mm(gproj, w1g.T)
    gslot = return_rows(local_slot.reshape(window, cap, width)).reshape(window * cap, width)
    grid_grad = jnp.zeros((grid_lat.shape[0], width), f32).at[row_ids].add(gslot).astype(bf16)
    term = jnp.concatenate([term_e, term_g, term_m], axis=0)
    w1_grad = lax.psum_scatter(term, "band", scatter_dimension=0, tiled=True)
    return (mesh_new, grid_grad, w1_grad)


def slot_of(place, d, window):
    return (place - d + window // 2) & (window - 1)


def swap(array, k):
    return lax.ppermute(array, "band", [(i, i ^ k) for i in range(16)])


def exchange(blocks):
    return lax.all_to_all(blocks, "band", 0, 0, tiled=True)


def start_all(copies):
    for copy in copies:
        copy.start()
    return copies


def gather_kernel(ids_hbm, grid_hbm, out_hbm, ids_ref, grid_ref, sel_ref, out_ref, sems):
    window, cap = ids_ref.shape[1:]
    ids_copy, grid_copy = start_all(
        [
            pltpu.make_async_copy(ids_hbm, ids_ref, sems.at[0]),
            pltpu.make_async_copy(grid_hbm, grid_ref, sems.at[1]),
        ]
    )
    d = lax.axis_index("band")
    lane = lax.broadcasted_iota(jnp.int32, (cap, window), 1)
    column = lax.broadcasted_iota(jnp.int32, (cap, grid_ref.shape[0]), 1)
    ids_copy.wait()
    table = jnp.transpose(ids_ref[0].astype(f32))
    for place in range(window):
        mine = jnp.where(lane == slot_of(place, d, window), table, 0.0)
        ids = jnp.sum(mine, axis=1, keepdims=True).astype(jnp.int32)
        sel_ref[place * cap : (place + 1) * cap] = (ids == column).astype(f32).astype(bf16)
    grid_copy.wait()
    rows = 256
    copies = []
    for i in range(out_ref.shape[0] // rows):
        part = slice(i * rows, (i + 1) * rows)
        out_ref[part] = mm(sel_ref[part], grid_ref[...]).astype(bf16)
        copies += start_all([pltpu.make_async_copy(out_ref.at[part], out_hbm.at[part], sems.at[2 + i])])
    for copy in copies:
        copy.wait()


def gather(send_rows, grid_lat):
    window, cap = send_rows.shape[1:]
    shape = (window * cap, grid_lat.shape[1])
    return pl.pallas_call(
        gather_kernel,
        out_shape=jax.ShapeDtypeStruct(shape, bf16),
        in_specs=[HBM, HBM],
        out_specs=HBM,
        scratch_shapes=[
            pltpu.VMEM(send_rows.shape, jnp.int32),
            pltpu.VMEM(grid_lat.shape, bf16),
            pltpu.VMEM((shape[0], grid_lat.shape[0]), bf16),
            pltpu.VMEM(shape, bf16),
            pltpu.SemaphoreType.DMA((2 + shape[0] // 256,)),
        ],
        compiler_params=pltpu.CompilerParams(vmem_limit_bytes=VMEM),
        cost_estimate=QUICK,
        name="gather_rows",
    )(send_rows, grid_lat)


def own_kernel(
    edges_hbm, mesh_hbm, w1_hbm, out_hbm, pre_hbm,
    edges_ref, mesh_ref, w1_ref, out_ref, pre_ref, sem,
):
    width = edges_ref.shape[1]
    nodes = mesh_ref.shape[0]
    slots = edges_ref.shape[0] // nodes
    few = 16
    block = few * slots
    blocks = nodes // few
    loads = [
        pltpu.make_async_copy(
            edges_hbm.at[i * block : (i + 1) * block], edges_ref.at[i * block : (i + 1) * block], sem.at[i]
        )
        for i in range(blocks)
    ]
    loads += [
        pltpu.make_async_copy(mesh_hbm, mesh_ref, sem.at[blocks]),
        pltpu.make_async_copy(w1_hbm.at[:width], w1_ref.at[:width], sem.at[blocks + 1]),
        pltpu.make_async_copy(w1_hbm.at[2 * width :], w1_ref.at[width:], sem.at[blocks + 2]),
    ]
    start_all(loads)
    to = lax.broadcasted_iota(jnp.int32, (block, block), 0)
    at = lax.broadcasted_iota(jnp.int32, (block, block), 1)
    turn = (at == (to % few) * slots + to // few).astype(f32).astype(bf16)
    for i in range(blocks):
        loads[i].wait()
        rows = mm(turn, edges_ref[i * block : (i + 1) * block]).astype(bf16)
        for k in range(slots):
            out_ref[k * nodes + i * few : k * nodes + (i + 1) * few] = rows[k * few : (k + 1) * few]
    copies = start_all([pltpu.make_async_copy(out_ref, out_hbm, sem.at[0])])
    for copy in loads[blocks:]:
        copy.wait()
    for k in range(slots):
        part = slice(k * nodes, (k + 1) * nodes)
        both = jnp.concatenate([out_ref[part], mesh_ref[...]], axis=1)
        pre_ref[part] = mm(both, w1_ref[...])
        copies += start_all(
            [pltpu.make_async_copy(pre_ref.at[part], pre_hbm.at[part], sem.at[blocks + 3 + k])]
        )
    for copy in copies:
        copy.wait()


def own(edges, mesh_lat, w1):
    total, width = edges.shape
    sd = jax.ShapeDtypeStruct
    nodes = mesh_lat.shape[0]
    return pl.pallas_call(
        own_kernel,
        out_shape=[sd((total, width), bf16), sd((total, width), f32)],
        in_specs=[HBM] * 3,
        out_specs=[HBM] * 2,
        scratch_shapes=[
            pltpu.VMEM((total, width), bf16),
            pltpu.VMEM(mesh_lat.shape, bf16),
            pltpu.VMEM((2 * width, width), bf16),
            pltpu.VMEM((total, width), bf16),
            pltpu.VMEM((total, width), f32),
            pltpu.SemaphoreType.DMA((nodes // 16 + 3 + total // nodes,)),
        ],
        compiler_params=pltpu.CompilerParams(vmem_limit_bytes=VMEM),
        cost_estimate=QUICK,
        name="own_terms",
    )(edges, mesh_lat, w1)


def sigmoid(v):
    return 1.0 / (1.0 + jnp.exp(-v))


def row_mean(v):
    return jnp.mean(v, axis=-1, keepdims=True)


STEP = 256


def slot_places(src, window, cap):
    d = lax.axis_index("band")
    return ((d - src // cap + window // 2) & (window - 1)) * cap + (src & (cap - 1))


def middle_kernel(
    window, pre_hbm, edges_hbm, arrived_hbm, w1_hbm, w2_hbm, mesh_hbm, cot_hbm, v1_hbm, n2_hbm,
    mask_hbm, src_hbm,
    new_hbm, gslot_hbm, keep_hbm, send_hbm,
    pre, edges_ref, arrived_ref, w1g_ref, w2_ref, mesh_ref, cot_ref, v1_ref, n2_ref, mask_ref,
    src_ref, new_ref, gslot_ref, send_ref,
    proj, dsilu, hn, rm, agg, g1_ref, gproj_ref, term, sems,
):
    width = w2_ref.shape[0]
    nodes = mesh_ref.shape[0]
    total = pre_hbm.shape[0]
    steps = total // STEP
    per = STEP // nodes
    cap = arrived_ref.shape[0] // window
    small = [
        (w1_hbm.at[width : 2 * width], w1g_ref), (arrived_hbm, arrived_ref), (src_hbm, src_ref),
        (mask_hbm, mask_ref), (w2_hbm, w2_ref),
        (mesh_hbm, mesh_ref), (v1_hbm, v1_ref), (n2_hbm, n2_ref), (cot_hbm, cot_ref),
        (edges_hbm, edges_ref),
    ]
    small = [pltpu.make_async_copy(*pair, sems.at[i]) for i, pair in enumerate(small)]
    loads = []
    for i in range(steps):
        part = slice(i * STEP, (i + 1) * STEP)
        loads.append(pltpu.make_async_copy(pre_hbm.at[part], pre.at[part], sems.at[len(small) + i]))
    start_all(small[:5] + loads + small[5:])
    for copy in small[:2]:
        copy.wait()
    proj[...] = mm(arrived_ref[...], w1g_ref[...]).astype(bf16)
    for copy in small[2:5]:
        copy.wait()
    place = slot_places(src_ref[...], window, cap).astype(f32)
    both = jnp.transpose(jnp.concatenate([place, mask_ref[...].astype(f32)], axis=0))
    slots = place.shape[0]
    column = lax.broadcasted_iota(jnp.int32, (nodes, proj.shape[0]), 1)
    agg[...] = jnp.zeros_like(agg)
    for i in range(steps):
        part = slice(i * STEP, (i + 1) * STEP)
        hot = jnp.concatenate(
            [
                (both[:, k : k + 1].astype(jnp.int32) == column).astype(f32).astype(bf16)
                for k in range(i * per, (i + 1) * per)
            ],
            axis=0,
        )
        got = mm(hot, proj[...])
        loads[i].wait()
        v = pre[part] + got
        sig = sigmoid(v)
        hid = v * sig
        dsilu[part] = sig + hid * (1.0 - sig)
        p2 = mm(hid.astype(bf16), w2_ref[...])
        c = p2 - row_mean(p2)
        r = lax.rsqrt(row_mean(c * c) + eps)
        h = c * r
        hn[part] = h
        m = jnp.concatenate(
            [both[:, slots + k : slots + k + 1] for k in range(i * per, (i + 1) * per)], axis=0
        )
        rm[part] = r * m
        msg = h * m
        add = msg[:nodes]
        for n in range(1, per):
            add = add + msg[n * nodes : (n + 1) * nodes]
        agg[...] += add
    for copy in small[5:]:
        copy.wait()
    mesh = mesh_ref[...]
    p3 = mm(mesh, v1_ref[:width]) + mm(agg[...].astype(bf16), v1_ref[width:])
    sig = sigmoid(p3)
    a3 = p3 * sig
    p4 = mm(a3.astype(bf16), n2_ref[...])
    c = p4 - row_mean(p4)
    r = lax.rsqrt(row_mean(c * c) + eps)
    h = c * r
    new_ref[...] = (mesh.astype(f32) + h).astype(bf16)
    stores = start_all([pltpu.make_async_copy(new_ref, new_hbm, sems.at[0])])
    cot = cot_ref[...].astype(f32)
    g4 = (r * (cot - row_mean(cot) - h * row_mean(cot * h))).astype(bf16)
    g3 = (mm_t(g4, n2_ref[...]) * (sig + a3 * (1.0 - sig))).astype(bf16)
    ga = mm_t(g3, v1_ref[width:])
    agg[...] = ga - row_mean(ga)
    for i in range(steps):
        part = slice(i * STEP, (i + 1) * STEP)
        ga = jnp.concatenate([agg[...]] * per, axis=0)
        h = hn[part]
        g2 = rm[part] * (ga - h * row_mean(ga * h))
        g1_ref[part] = (mm_t(g2.astype(bf16), w2_ref[...]) * dsilu[part]).astype(bf16)
    src = slot_places(src_ref[...], window, cap)
    rows = 256
    for i in range(gproj_ref.shape[0] // rows):
        part = slice(i * rows, (i + 1) * rows)
        slot = lax.broadcasted_iota(jnp.int32, (rows, nodes), 0) + i * rows
        sel = jnp.concatenate(
            [(slot == src[k : k + 1]).astype(f32).astype(bf16) for k in range(slots)], axis=1
        )
        gp = mm(sel, g1_ref[...]).astype(bf16)
        gproj_ref[part] = gp
        gslot_ref[part] = mm_t(gp, w1g_ref[...]).astype(bf16)
        stores += start_all(
            [pltpu.make_async_copy(gslot_ref.at[part], gslot_hbm.at[part], sems.at[1 + i])]
        )
    g1 = g1_ref[...]
    term[:width] = outer_sum(edges_ref[...], g1)
    term[width : 2 * width] = outer_sum(arrived_ref[...], gproj_ref[...])
    gsum = g1[:nodes].astype(f32)
    for k in range(1, slots):
        gsum = gsum + g1[k * nodes : (k + 1) * nodes].astype(f32)
    term[2 * width :] = outer_sum(mesh_ref[...], gsum.astype(bf16))
    share = send_ref.shape[1]
    d = lax.axis_index("band")
    at = len(stores)
    for i, k in enumerate(SHARE):
        rows = pl.ds(pl.multiple_of((d ^ k) * share, share), share)
        stores += start_all([pltpu.make_async_copy(term.at[rows], keep_hbm.at[i], sems.at[at + i])])
    for i, k in enumerate(SHARE):
        rows = pl.ds(pl.multiple_of((d ^ k ^ 1) * share, share), share)
        send_ref[i] = term[rows].astype(bf16)
    stores += start_all([pltpu.make_async_copy(send_ref, send_hbm, sems.at[at + len(SHARE)])])
    for copy in stores:
        copy.wait()


SHARE = [4 * kz + 2 * ky for ky in range(2) for kz in range(4)]


def middle(window, pre, edges, arrived, w1, w2, mesh_lat, cot, v1, n2, mask, src):
    total, width = pre.shape
    nodes = mesh_lat.shape[0]
    sd = jax.ShapeDtypeStruct
    vm = pltpu.VMEM
    share = (len(SHARE), 3 * width // 16, width)
    return pl.pallas_call(
        functools.partial(middle_kernel, window),
        out_shape=[sd((nodes, width), bf16), sd(arrived.shape, bf16), sd(share, f32), sd(share, bf16)],
        in_specs=[HBM] * 11,
        out_specs=[HBM] * 4,
        scratch_shapes=[
            vm((total, width), f32),
            vm((total, width), bf16),
            vm(arrived.shape, bf16),
            vm(w2.shape, bf16),
            vm(w2.shape, bf16),
            vm(mesh_lat.shape, bf16),
            vm(cot.shape, bf16),
            vm(v1.shape, bf16),
            vm(n2.shape, bf16),
            vm(mask.shape, jnp.int32),
            vm(src.shape, jnp.int32),
            vm(mesh_lat.shape, bf16),
            vm(arrived.shape, bf16),
            vm(share, bf16),
            vm(arrived.shape, bf16),
            vm((total, width), f32),
            vm((total, width), f32),
            vm((total, 1), f32),
            vm((nodes, width), f32),
            vm((total, width), bf16),
            vm(arrived.shape, bf16),
            vm((3 * width, width), f32),
            pltpu.SemaphoreType.DMA((10 + total // STEP,)),
        ],
        compiler_params=pltpu.CompilerParams(vmem_limit_bytes=VMEM),
        cost_estimate=QUICK,
        name="edges_and_nodes",
    )(pre, edges, arrived, w1, w2, mesh_lat, cot, v1, n2, mask, src)


def share_sum(keep, send):
    keep = keep + swap(send, 1).astype(f32)
    half = keep.shape[0] // 2
    keep = keep[:half] + swap(keep[half:].astype(bf16), 2).astype(f32)
    send = keep.astype(bf16)
    others = [swap(send[kz], 4 * kz) for kz in (2, 3, 1)]
    return keep[0], others


def grid_kernel(ids_ref, rows_ref, out_ref, at_ref):
    window, cap = ids_ref.shape[1:]
    d = lax.axis_index("band")
    for place in range(window):
        at_ref[:, place * cap : (place + 1) * cap] = ids_ref[0, pl.ds(slot_of(place, d, window), 1), :]
    ids = at_ref[...]
    block = 256
    for i in range(out_ref.shape[0] // block):
        row = lax.broadcasted_iota(jnp.int32, (block, ids.shape[1]), 0) + i * block
        sel = (row == ids).astype(f32).astype(bf16)
        out_ref[i * block : (i + 1) * block] = mm(sel, rows_ref[...]).astype(bf16)


def grid_sum(send_rows, rows, grid_rows):
    slots, width = rows.shape
    return pl.pallas_call(
        grid_kernel,
        out_shape=jax.ShapeDtypeStruct((grid_rows, width), bf16),
        in_specs=[VM] * 2,
        out_specs=VM,
        scratch_shapes=[pltpu.VMEM((1, slots), jnp.int32)],
        compiler_params=pltpu.CompilerParams(vmem_limit_bytes=10 << 20),
        cost_estimate=pl.CostEstimate(
            flops=2 * grid_rows * slots * width, bytes_accessed=4 << 20, transcendentals=0
        ),
        name="grid_sum",
    )(send_rows, rows)


def per_device_all(
    grid_lat, mesh_lat, edge_lat, edge_w1, edge_w2, node_w1, node_w2, mesh_cot,
    send_rows, edge_src, edge_mask,
):
    width = mesh_lat.shape[1]
    nodes, slots = edge_src.shape
    arrived = exchange(gather(send_rows, grid_lat))

    edges, pre = own(edge_lat.reshape(nodes * slots, width), mesh_lat, edge_w1)
    src = jnp.transpose(edge_src)
    mask = jnp.transpose(edge_mask)

    mesh_new, gslot, keep, send = middle(
        send_rows.shape[1], pre, edges, arrived, edge_w1, edge_w2, mesh_lat, mesh_cot, node_w1,
        node_w2, mask, src,
    )
    returned = exchange(gslot)
    mine, others = share_sum(keep, send)
    grid_grad = grid_sum(send_rows, returned, grid_lat.shape[0])
    grid_grad, mine = lax.optimization_barrier((grid_grad, mine))
    w1_grad = mine
    for other in others:
        w1_grad = w1_grad + other.astype(f32)
    return (mesh_new, grid_grad, w1_grad)


def solution(mesh):
    in_specs = (
        P(("group", "band"), None),
        P(("group", "band"), None),
        P(("group", "band"), None, None),
        P(),
        P(),
        P(),
        P(),
        P(("group", "band"), None),
        P("band", None, None),
        P("band", None),
        P("band", None),
    )
    out_specs = (P(("group", "band"), None), P(("group", "band"), None), P(("group", "band"), None))

    def step(*args):
        window = args[8].shape[1]
        every = mesh.shape["band"] == window == 16
        body = per_device_all if every else per_device_window
        return jax.shard_map(
            body, mesh=mesh, in_specs=in_specs, out_specs=out_specs, check_vma=False
        )(*args)

    return step
```

```python
import functools

import jax
import jax.numpy as jnp
from jax import lax
from jax.experimental import pallas as pl
from jax.experimental.pallas import tpu as pltpu
from jax.sharding import PartitionSpec as P

eps = 1e-05
f32 = jnp.float32
bf16 = jnp.bfloat16
VM = pl.BlockSpec(memory_space=pltpu.VMEM)
HBM = pl.BlockSpec(memory_space=pltpu.HBM)
VMEM = 56 << 20
QUICK = pl.CostEstimate(flops=1, bytes_accessed=1, transcendentals=0)


def from_behind(array, axis, by):
    devices = lax.axis_size(axis)
    return lax.ppermute(array, axis, [(i, (i + by) % devices) for i in range(devices)])


def layer_norm(value):
    centred = value - jnp.mean(value, axis=-1, keepdims=True)
    scale = lax.rsqrt(jnp.mean(centred * centred, axis=-1, keepdims=True) + eps)
    return centred * scale


def norm_back(value, grad):
    centred = value - jnp.mean(value, axis=-1, keepdims=True)
    scale = lax.rsqrt(jnp.mean(centred * centred, axis=-1, keepdims=True) + eps)
    normed = centred * scale
    return scale * (
        grad
        - jnp.mean(grad, axis=-1, keepdims=True)
        - normed * jnp.mean(grad * normed, axis=-1, keepdims=True)
    )


def silu_grad(value):
    sig = jax.nn.sigmoid(value)
    return sig * (1.0 + value * (1.0 - sig))


def outer_sum(left, right):
    return lax.dot_general(
        left, right, (((0,), (0,)), ((), ())), preferred_element_type=f32
    )


def mm(left, right):
    return jnp.dot(left, right, preferred_element_type=f32)


def mm_t(left, right):
    return lax.dot_general(
        left, right, (((1,), (1,)), ((), ())), preferred_element_type=f32
    )


def send_forward(outgoing):
    window = outgoing.shape[0]
    half = window // 2
    pieces = []
    for slot in range(window):
        offset = slot - half
        if offset == 0:
            pieces.append(outgoing[slot])
        else:
            pieces.append(from_behind(outgoing[slot], "band", offset))
    return jnp.stack(pieces, axis=0)


def return_rows(grads):
    window = grads.shape[0]
    half = window // 2
    pieces = []
    for slot in range(window):
        offset = slot - half
        if offset == 0:
            pieces.append(grads[slot])
        else:
            pieces.append(
                from_behind(grads[slot].astype(bf16), "band", -offset).astype(f32)
            )
    return jnp.stack(pieces, axis=0)


def per_device_window(
    grid_lat, mesh_lat, edge_lat, edge_w1, edge_w2, node_w1, node_w2, mesh_cot,
    send_rows, edge_src, edge_mask,
):
    width = mesh_lat.shape[1]
    nodes, slots = edge_src.shape
    window = send_rows.shape[1]
    cap = send_rows.shape[2]
    w1e = edge_w1[:width]
    w1g = edge_w1[width : 2 * width]
    w1m = edge_w1[2 * width :]
    v1m = node_w1[:width]
    v1a = node_w1[width:]
    row_ids = send_rows[0].reshape(-1)
    outgoing_raw = grid_lat[row_ids]
    arrived = send_forward(outgoing_raw.reshape(window, cap, width)).reshape(window * cap, width)
    proj = mm(arrived, w1g).astype(bf16)
    flat_src = edge_src.reshape(-1)
    edges = edge_lat.reshape(nodes * slots, width)
    mesh_rep = jnp.repeat(mesh_lat, slots, axis=0)
    maskf = edge_mask.reshape(-1, 1).astype(f32)
    pre1 = mm(edges, w1e) + mm(mesh_rep, w1m) + proj[flat_src].astype(f32)
    hid = jax.nn.silu(pre1).astype(bf16)
    pre2 = mm(hid, edge_w2)
    msg = layer_norm(pre2) * maskf
    agg = jnp.sum(msg.reshape(nodes, slots, width), axis=1).astype(bf16)
    pre3 = mm(mesh_lat, v1m) + mm(agg, v1a)
    act = jax.nn.silu(pre3).astype(bf16)
    pre4 = mm(act, node_w2)
    mesh_new = (mesh_lat.astype(f32) + layer_norm(pre4)).astype(bf16)
    g4 = norm_back(pre4, mesh_cot.astype(f32)).astype(bf16)
    g3 = (mm(g4, node_w2.T) * silu_grad(pre3)).astype(bf16)
    gagg = mm(g3, v1a.T)
    g2 = norm_back(pre2, jnp.repeat(gagg, slots, axis=0) * maskf).astype(bf16)
    g1 = (mm(g2, edge_w2.T) * silu_grad(pre1)).astype(bf16)
    gproj = jnp.zeros((window * cap, width), f32).at[flat_src].add(g1.astype(f32)).astype(bf16)
    term_e = outer_sum(edges, g1)
    term_m = outer_sum(mesh_rep, g1)
    term_g = outer_sum(arrived, gproj)
    local_slot = mm(gproj, w1g.T)
    gslot = return_rows(local_slot.reshape(window, cap, width)).reshape(window * cap, width)
    grid_grad = jnp.zeros((grid_lat.shape[0], width), f32).at[row_ids].add(gslot).astype(bf16)
    term = jnp.concatenate([term_e, term_g, term_m], axis=0)
    w1_grad = lax.psum_scatter(term, "band", scatter_dimension=0, tiled=True)
    return (mesh_new, grid_grad, w1_grad)


def slot_of(place, d, window):
    return (place - d + window // 2) & (window - 1)


def swap(array, k):
    return lax.ppermute(array, "band", [(i, i ^ k) for i in range(16)])


def exchange(blocks):
    return lax.all_to_all(blocks, "band", 0, 0, tiled=True)


def start_all(copies):
    for copy in copies:
        copy.start()
    return copies


GATHER = 256


def gather_kernel(ids_hbm, grid_hbm, out_hbm, ids_ref, grid_ref, sel_ref, out_ref, sems):
    window, cap = ids_ref.shape[1:]
    ids_copy, grid_copy = start_all(
        [
            pltpu.make_async_copy(ids_hbm, ids_ref, sems.at[0]),
            pltpu.make_async_copy(grid_hbm, grid_ref, sems.at[1]),
        ]
    )
    d = lax.axis_index("band")
    lane = lax.broadcasted_iota(jnp.int32, (cap, window), 1)
    column = lax.broadcasted_iota(jnp.int32, (cap, grid_ref.shape[0]), 1)
    ids_copy.wait()
    table = jnp.transpose(ids_ref[0].astype(f32))
    rows = GATHER
    copies = []
    for i in range(out_ref.shape[0] // rows):
        part = slice(i * rows, (i + 1) * rows)
        for place in range(i * rows // cap, (i + 1) * rows // cap):
            mine = jnp.where(lane == slot_of(place, d, window), table, 0.0)
            ids = jnp.sum(mine, axis=1, keepdims=True).astype(jnp.int32)
            sel_ref[place * cap : (place + 1) * cap] = (ids == column).astype(f32).astype(bf16)
        if i == 0:
            grid_copy.wait()
        out_ref[part] = mm(sel_ref[part], grid_ref[...]).astype(bf16)
        copies += start_all([pltpu.make_async_copy(out_ref.at[part], out_hbm.at[part], sems.at[2 + i])])
    for copy in copies:
        copy.wait()


def gather(send_rows, grid_lat):
    window, cap = send_rows.shape[1:]
    shape = (window * cap, grid_lat.shape[1])
    return pl.pallas_call(
        gather_kernel,
        out_shape=jax.ShapeDtypeStruct(shape, bf16),
        in_specs=[HBM, HBM],
        out_specs=HBM,
        scratch_shapes=[
            pltpu.VMEM(send_rows.shape, jnp.int32),
            pltpu.VMEM(grid_lat.shape, bf16),
            pltpu.VMEM((shape[0], grid_lat.shape[0]), bf16),
            pltpu.VMEM(shape, bf16),
            pltpu.SemaphoreType.DMA((2 + shape[0] // GATHER,)),
        ],
        compiler_params=pltpu.CompilerParams(vmem_limit_bytes=VMEM),
        cost_estimate=QUICK,
        name="gather_rows",
    )(send_rows, grid_lat)


def own_kernel(
    edges_hbm, mesh_hbm, w1_hbm, out_hbm, pre_hbm,
    edges_ref, mesh_ref, w1_ref, out_ref, pre_ref, sem,
):
    width = edges_ref.shape[1]
    nodes = mesh_ref.shape[0]
    slots = edges_ref.shape[0] // nodes
    few = 16
    block = few * slots
    blocks = nodes // few
    loads = [
        pltpu.make_async_copy(
            edges_hbm.at[i * block : (i + 1) * block], edges_ref.at[i * block : (i + 1) * block], sem.at[i]
        )
        for i in range(blocks)
    ]
    loads += [
        pltpu.make_async_copy(mesh_hbm, mesh_ref, sem.at[blocks]),
        pltpu.make_async_copy(w1_hbm.at[:width], w1_ref.at[:width], sem.at[blocks + 1]),
        pltpu.make_async_copy(w1_hbm.at[2 * width :], w1_ref.at[width:], sem.at[blocks + 2]),
    ]
    start_all(loads)
    to = lax.broadcasted_iota(jnp.int32, (block, block), 0)
    at = lax.broadcasted_iota(jnp.int32, (block, block), 1)
    turn = (at == (to % few) * slots + to // few).astype(f32).astype(bf16)
    for i in range(blocks):
        loads[i].wait()
        rows = mm(turn, edges_ref[i * block : (i + 1) * block]).astype(bf16)
        for k in range(slots):
            out_ref[k * nodes + i * few : k * nodes + (i + 1) * few] = rows[k * few : (k + 1) * few]
    copies = start_all([pltpu.make_async_copy(out_ref, out_hbm, sem.at[0])])
    for copy in loads[blocks:]:
        copy.wait()
    for k in range(slots):
        part = slice(k * nodes, (k + 1) * nodes)
        both = jnp.concatenate([out_ref[part], mesh_ref[...]], axis=1)
        pre_ref[part] = mm(both, w1_ref[...])
        copies += start_all(
            [pltpu.make_async_copy(pre_ref.at[part], pre_hbm.at[part], sem.at[blocks + 3 + k])]
        )
    for copy in copies:
        copy.wait()


def own(edges, mesh_lat, w1):
    total, width = edges.shape
    sd = jax.ShapeDtypeStruct
    nodes = mesh_lat.shape[0]
    return pl.pallas_call(
        own_kernel,
        out_shape=[sd((total, width), bf16), sd((total, width), f32)],
        in_specs=[HBM] * 3,
        out_specs=[HBM] * 2,
        scratch_shapes=[
            pltpu.VMEM((total, width), bf16),
            pltpu.VMEM(mesh_lat.shape, bf16),
            pltpu.VMEM((2 * width, width), bf16),
            pltpu.VMEM((total, width), bf16),
            pltpu.VMEM((total, width), f32),
            pltpu.SemaphoreType.DMA((nodes // 16 + 3 + total // nodes,)),
        ],
        compiler_params=pltpu.CompilerParams(vmem_limit_bytes=VMEM),
        cost_estimate=QUICK,
        name="own_terms",
    )(edges, mesh_lat, w1)


def sigmoid(v):
    return 1.0 / (1.0 + jnp.exp(-v))


def row_mean(v):
    return jnp.mean(v, axis=-1, keepdims=True)


STEP = 512


def slot_places(src, window, cap):
    d = lax.axis_index("band")
    return ((d - src // cap + window // 2) & (window - 1)) * cap + (src & (cap - 1))


def middle_kernel(
    window, pre_hbm, arrived_hbm, w1_hbm, w2_hbm, mesh_hbm, cot_hbm, v1_hbm, n2_hbm,
    mask_hbm, src_hbm,
    new_hbm, gslot_hbm, gproj_hbm, g1_hbm,
    pre, arrived_ref, w1g_ref, w2_ref, mesh_ref, cot_ref, v1_ref, n2_ref, mask_ref,
    src_ref, new_ref, gslot_ref,
    proj, dsilu, hn, rm, agg, g1_ref, gproj_ref, sems,
):
    width = w2_ref.shape[0]
    nodes = mesh_ref.shape[0]
    total = pre_hbm.shape[0]
    steps = total // STEP
    per = STEP // nodes
    cap = arrived_ref.shape[0] // window
    small = [
        (w1_hbm.at[width : 2 * width], w1g_ref), (arrived_hbm, arrived_ref), (src_hbm, src_ref),
        (mask_hbm, mask_ref), (w2_hbm, w2_ref),
        (mesh_hbm, mesh_ref), (v1_hbm, v1_ref), (n2_hbm, n2_ref), (cot_hbm, cot_ref),
    ]
    small = [pltpu.make_async_copy(*pair, sems.at[i]) for i, pair in enumerate(small)]
    loads = []
    for i in range(steps):
        part = slice(i * STEP, (i + 1) * STEP)
        loads.append(pltpu.make_async_copy(pre_hbm.at[part], pre.at[part], sems.at[len(small) + i]))
    start_all(small[:2] + loads[:1] + small[2:5] + loads[1:] + small[5:])
    for copy in small[:2]:
        copy.wait()
    proj[...] = mm(arrived_ref[...], w1g_ref[...]).astype(bf16)
    for copy in small[2:5]:
        copy.wait()
    place = slot_places(src_ref[...], window, cap).astype(f32)
    both = jnp.transpose(jnp.concatenate([place, mask_ref[...].astype(f32)], axis=0))
    slots = place.shape[0]
    column = lax.broadcasted_iota(jnp.int32, (nodes, proj.shape[0]), 1)
    agg[...] = jnp.zeros_like(agg)
    for i in range(steps):
        part = slice(i * STEP, (i + 1) * STEP)
        hot = jnp.concatenate(
            [
                (both[:, k : k + 1].astype(jnp.int32) == column).astype(f32).astype(bf16)
                for k in range(i * per, (i + 1) * per)
            ],
            axis=0,
        )
        got = mm(hot, proj[...])
        loads[i].wait()
        v = pre[part] + got
        sig = sigmoid(v)
        hid = v * sig
        dsilu[part] = sig + hid * (1.0 - sig)
        p2 = mm(hid.astype(bf16), w2_ref[...])
        c = p2 - row_mean(p2)
        r = lax.rsqrt(row_mean(c * c) + eps)
        h = c * r
        hn[part] = h
        m = jnp.concatenate(
            [both[:, slots + k : slots + k + 1] for k in range(i * per, (i + 1) * per)], axis=0
        )
        rm[part] = r * m
        msg = h * m
        add = msg[:nodes]
        for n in range(1, per):
            add = add + msg[n * nodes : (n + 1) * nodes]
        agg[...] += add
    for copy in small[5:]:
        copy.wait()
    mesh = mesh_ref[...]
    p3 = mm(mesh, v1_ref[:width]) + mm(agg[...].astype(bf16), v1_ref[width:])
    sig = sigmoid(p3)
    a3 = p3 * sig
    p4 = mm(a3.astype(bf16), n2_ref[...])
    c = p4 - row_mean(p4)
    r = lax.rsqrt(row_mean(c * c) + eps)
    h = c * r
    new_ref[...] = (mesh.astype(f32) + h).astype(bf16)
    stores = start_all([pltpu.make_async_copy(new_ref, new_hbm, sems.at[0])])
    cot = cot_ref[...].astype(f32)
    g4 = (r * (cot - row_mean(cot) - h * row_mean(cot * h))).astype(bf16)
    g3 = (mm_t(g4, n2_ref[...]) * (sig + a3 * (1.0 - sig))).astype(bf16)
    ga = mm_t(g3, v1_ref[width:])
    agg[...] = ga - row_mean(ga)
    for i in range(steps):
        part = slice(i * STEP, (i + 1) * STEP)
        ga = jnp.concatenate([agg[...]] * per, axis=0)
        h = hn[part]
        g2 = rm[part] * (ga - h * row_mean(ga * h))
        g1_ref[part] = (mm_t(g2.astype(bf16), w2_ref[...]) * dsilu[part]).astype(bf16)
    stores += start_all([pltpu.make_async_copy(g1_ref, g1_hbm, sems.at[1])])
    src = slot_places(src_ref[...], window, cap)
    rows = 256
    for i in range(gproj_ref.shape[0] // rows):
        part = slice(i * rows, (i + 1) * rows)
        slot = lax.broadcasted_iota(jnp.int32, (rows, nodes), 0) + i * rows
        sel = jnp.concatenate(
            [(slot == src[k : k + 1]).astype(f32).astype(bf16) for k in range(slots)], axis=1
        )
        gp = mm(sel, g1_ref[...]).astype(bf16)
        gproj_ref[part] = gp
        gslot_ref[part] = mm_t(gp, w1g_ref[...]).astype(bf16)
        stores += start_all(
            [
                pltpu.make_async_copy(gslot_ref.at[part], gslot_hbm.at[part], sems.at[2 + i]),
                pltpu.make_async_copy(gproj_ref.at[part], gproj_hbm.at[part], sems.at[6 + i]),
            ]
        )
    for copy in stores:
        copy.wait()


SHARE = [4 * kz + 2 * ky for ky in range(2) for kz in range(4)]
PIECES = 4


def middle(window, pre, arrived, w1, w2, mesh_lat, cot, v1, n2, mask, src):
    total, width = pre.shape
    nodes = mesh_lat.shape[0]
    sd = jax.ShapeDtypeStruct
    vm = pltpu.VMEM
    return pl.pallas_call(
        functools.partial(middle_kernel, window),
        out_shape=[
            sd((nodes, width), bf16), sd(arrived.shape, bf16), sd(arrived.shape, bf16),
            sd((total, width), bf16),
        ],
        in_specs=[HBM] * 10,
        out_specs=[HBM] * 4,
        scratch_shapes=[
            vm((total, width), f32),
            vm(arrived.shape, bf16),
            vm(w2.shape, bf16),
            vm(w2.shape, bf16),
            vm(mesh_lat.shape, bf16),
            vm(cot.shape, bf16),
            vm(v1.shape, bf16),
            vm(n2.shape, bf16),
            vm(mask.shape, jnp.int32),
            vm(src.shape, jnp.int32),
            vm(mesh_lat.shape, bf16),
            vm(arrived.shape, bf16),
            vm(arrived.shape, bf16),
            vm((total, width), f32),
            vm((total, width), f32),
            vm((total, 1), f32),
            vm((nodes, width), f32),
            vm((total, width), bf16),
            vm(arrived.shape, bf16),
            pltpu.SemaphoreType.DMA((10 + total // STEP,)),
        ],
        compiler_params=pltpu.CompilerParams(vmem_limit_bytes=VMEM),
        cost_estimate=QUICK,
        name="edges_and_nodes",
    )(pre, arrived, w1, w2, mesh_lat, cot, v1, n2, mask, src)


def terms_kernel(edges_ref, g1_ref, mesh_ref, arrived_ref, gproj_ref, *rest):
    keep, send, term = rest[:PIECES], rest[PIECES:-1], rest[-1]
    width = g1_ref.shape[1]
    nodes = mesh_ref.shape[0]
    g1 = g1_ref[...]
    term[:width] = outer_sum(edges_ref[...], g1)
    term[width : 2 * width] = outer_sum(arrived_ref[...], gproj_ref[...])
    gsum = g1[:nodes].astype(f32)
    for k in range(1, g1.shape[0] // nodes):
        gsum = gsum + g1[k * nodes : (k + 1) * nodes].astype(f32)
    term[2 * width :] = outer_sum(mesh_ref[...], gsum.astype(bf16))
    share = keep[0].shape[1]
    d = lax.axis_index("band")
    for i, k in enumerate(SHARE):
        at = pl.ds(pl.multiple_of((d ^ k ^ 1) * share, share), share)
        send[i // 2][i % 2] = term[at].astype(bf16)
    for i, k in enumerate(SHARE):
        at = pl.ds(pl.multiple_of((d ^ k) * share, share), share)
        keep[i // 2][i % 2] = term[at]


def terms(edges, g1, mesh_lat, arrived, gproj):
    width = g1.shape[1]
    share = (2, 3 * width // 16, width)
    sd = jax.ShapeDtypeStruct
    out = pl.pallas_call(
        terms_kernel,
        out_shape=[sd(share, f32)] * PIECES + [sd(share, bf16)] * PIECES,
        in_specs=[VM] * 5,
        out_specs=[VM] * (2 * PIECES),
        scratch_shapes=[pltpu.VMEM((3 * width, width), f32)],
        compiler_params=pltpu.CompilerParams(vmem_limit_bytes=16 << 20),
        cost_estimate=QUICK,
        name="w1_terms",
    )(edges, g1, mesh_lat, arrived, gproj)
    return out[:PIECES], out[PIECES:]


def share_sum(keep, send):
    full = [mine + swap(other, 1).astype(f32) for mine, other in zip(keep, send)]
    half = len(full) // 2
    full = [mine + swap(other.astype(bf16), 2).astype(f32) for mine, other in zip(full, full[half:])]
    shares = [piece[i].astype(bf16) for piece in full for i in range(piece.shape[0])]
    return full[0][0], [swap(shares[kz], 4 * kz) for kz in (2, 3, 1)]


def grid_kernel(ids_ref, rows_ref, out_ref, at_ref):
    window, cap = ids_ref.shape[1:]
    d = lax.axis_index("band")
    for place in range(window):
        at_ref[:, place * cap : (place + 1) * cap] = ids_ref[0, pl.ds(slot_of(place, d, window), 1), :]
    ids = at_ref[...]
    block = 256
    for i in range(out_ref.shape[0] // block):
        row = lax.broadcasted_iota(jnp.int32, (block, ids.shape[1]), 0) + i * block
        sel = (row == ids).astype(f32).astype(bf16)
        out_ref[i * block : (i + 1) * block] = mm(sel, rows_ref[...]).astype(bf16)


def grid_sum(send_rows, rows, grid_rows):
    slots, width = rows.shape
    return pl.pallas_call(
        grid_kernel,
        out_shape=jax.ShapeDtypeStruct((grid_rows, width), bf16),
        in_specs=[VM] * 2,
        out_specs=VM,
        scratch_shapes=[pltpu.VMEM((1, slots), jnp.int32)],
        compiler_params=pltpu.CompilerParams(vmem_limit_bytes=10 << 20),
        cost_estimate=pl.CostEstimate(
            flops=60 * grid_rows * slots * width, bytes_accessed=4 << 20, transcendentals=0
        ),
        name="grid_sum",
    )(send_rows, rows)


def per_device_all(
    grid_lat, mesh_lat, edge_lat, edge_w1, edge_w2, node_w1, node_w2, mesh_cot,
    send_rows, edge_src, edge_mask,
):
    width = mesh_lat.shape[1]
    nodes, slots = edge_src.shape
    arrived = exchange(gather(send_rows, grid_lat))

    edges, pre = own(edge_lat.reshape(nodes * slots, width), mesh_lat, edge_w1)
    src = jnp.transpose(edge_src)
    mask = jnp.transpose(edge_mask)

    mesh_new, gslot, gproj, g1 = middle(
        send_rows.shape[1], pre, arrived, edge_w1, edge_w2, mesh_lat, mesh_cot, node_w1,
        node_w2, mask, src,
    )
    returned = exchange(gslot)
    keep, send = terms(edges, g1, mesh_lat, arrived, gproj)
    mine, others = share_sum(keep, send)
    grid_grad = grid_sum(send_rows, returned, grid_lat.shape[0])
    grid_grad, w1_grad = lax.optimization_barrier((grid_grad, mine))
    for other in others:
        w1_grad = w1_grad + other.astype(f32)
    return (mesh_new, grid_grad, w1_grad)


def solution(mesh):
    in_specs = (
        P(("group", "band"), None),
        P(("group", "band"), None),
        P(("group", "band"), None, None),
        P(),
        P(),
        P(),
        P(),
        P(("group", "band"), None),
        P("band", None, None),
        P("band", None),
        P("band", None),
    )
    out_specs = (P(("group", "band"), None), P(("group", "band"), None), P(("group", "band"), None))

    def step(*args):
        window = args[8].shape[1]
        every = mesh.shape["band"] == window == 16
        body = per_device_all if every else per_device_window
        return jax.shard_map(
            body, mesh=mesh, in_specs=in_specs, out_specs=out_specs, check_vma=False
        )(*args)

    return step
```

```python
import functools

import jax
import jax.numpy as jnp
from jax import lax
from jax.experimental import pallas as pl
from jax.experimental.pallas import tpu as pltpu
from jax.sharding import PartitionSpec as P

eps = 1e-05
f32 = jnp.float32
bf16 = jnp.bfloat16
VM = pl.BlockSpec(memory_space=pltpu.VMEM)
HBM = pl.BlockSpec(memory_space=pltpu.HBM)
VMEM = 63 << 20
QUICK = pl.CostEstimate(flops=1, bytes_accessed=1, transcendentals=0)


def from_behind(array, axis, by):
    devices = lax.axis_size(axis)
    return lax.ppermute(array, axis, [(i, (i + by) % devices) for i in range(devices)])


def layer_norm(value):
    centred = value - jnp.mean(value, axis=-1, keepdims=True)
    scale = lax.rsqrt(jnp.mean(centred * centred, axis=-1, keepdims=True) + eps)
    return centred * scale


def norm_back(value, grad):
    centred = value - jnp.mean(value, axis=-1, keepdims=True)
    scale = lax.rsqrt(jnp.mean(centred * centred, axis=-1, keepdims=True) + eps)
    normed = centred * scale
    return scale * (
        grad
        - jnp.mean(grad, axis=-1, keepdims=True)
        - normed * jnp.mean(grad * normed, axis=-1, keepdims=True)
    )


def silu_grad(value):
    sig = jax.nn.sigmoid(value)
    return sig * (1.0 + value * (1.0 - sig))


def outer_sum(left, right):
    return lax.dot_general(
        left, right, (((0,), (0,)), ((), ())), preferred_element_type=f32
    )


def mm(left, right):
    return jnp.dot(left, right, preferred_element_type=f32)


def mm_t(left, right):
    return lax.dot_general(
        left, right, (((1,), (1,)), ((), ())), preferred_element_type=f32
    )


def send_forward(outgoing):
    window = outgoing.shape[0]
    half = window // 2
    pieces = []
    for slot in range(window):
        offset = slot - half
        if offset == 0:
            pieces.append(outgoing[slot])
        else:
            pieces.append(from_behind(outgoing[slot], "band", offset))
    return jnp.stack(pieces, axis=0)


def return_rows(grads):
    window = grads.shape[0]
    half = window // 2
    pieces = []
    for slot in range(window):
        offset = slot - half
        if offset == 0:
            pieces.append(grads[slot])
        else:
            pieces.append(
                from_behind(grads[slot].astype(bf16), "band", -offset).astype(f32)
            )
    return jnp.stack(pieces, axis=0)


def per_device_window(
    grid_lat, mesh_lat, edge_lat, edge_w1, edge_w2, node_w1, node_w2, mesh_cot,
    send_rows, edge_src, edge_mask,
):
    width = mesh_lat.shape[1]
    nodes, slots = edge_src.shape
    window = send_rows.shape[1]
    cap = send_rows.shape[2]
    w1e = edge_w1[:width]
    w1g = edge_w1[width : 2 * width]
    w1m = edge_w1[2 * width :]
    v1m = node_w1[:width]
    v1a = node_w1[width:]
    row_ids = send_rows[0].reshape(-1)
    outgoing_raw = grid_lat[row_ids]
    arrived = send_forward(outgoing_raw.reshape(window, cap, width)).reshape(window * cap, width)
    proj = mm(arrived, w1g).astype(bf16)
    flat_src = edge_src.reshape(-1)
    edges = edge_lat.reshape(nodes * slots, width)
    mesh_rep = jnp.repeat(mesh_lat, slots, axis=0)
    maskf = edge_mask.reshape(-1, 1).astype(f32)
    pre1 = mm(edges, w1e) + mm(mesh_rep, w1m) + proj[flat_src].astype(f32)
    hid = jax.nn.silu(pre1).astype(bf16)
    pre2 = mm(hid, edge_w2)
    msg = layer_norm(pre2) * maskf
    agg = jnp.sum(msg.reshape(nodes, slots, width), axis=1).astype(bf16)
    pre3 = mm(mesh_lat, v1m) + mm(agg, v1a)
    act = jax.nn.silu(pre3).astype(bf16)
    pre4 = mm(act, node_w2)
    mesh_new = (mesh_lat.astype(f32) + layer_norm(pre4)).astype(bf16)
    g4 = norm_back(pre4, mesh_cot.astype(f32)).astype(bf16)
    g3 = (mm(g4, node_w2.T) * silu_grad(pre3)).astype(bf16)
    gagg = mm(g3, v1a.T)
    g2 = norm_back(pre2, jnp.repeat(gagg, slots, axis=0) * maskf).astype(bf16)
    g1 = (mm(g2, edge_w2.T) * silu_grad(pre1)).astype(bf16)
    gproj = jnp.zeros((window * cap, width), f32).at[flat_src].add(g1.astype(f32)).astype(bf16)
    term_e = outer_sum(edges, g1)
    term_m = outer_sum(mesh_rep, g1)
    term_g = outer_sum(arrived, gproj)
    local_slot = mm(gproj, w1g.T)
    gslot = return_rows(local_slot.reshape(window, cap, width)).reshape(window * cap, width)
    grid_grad = jnp.zeros((grid_lat.shape[0], width), f32).at[row_ids].add(gslot).astype(bf16)
    term = jnp.concatenate([term_e, term_g, term_m], axis=0)
    w1_grad = lax.psum_scatter(term, "band", scatter_dimension=0, tiled=True)
    return (mesh_new, grid_grad, w1_grad)


def slot_of(place, d, window):
    return (place - d + window // 2) & (window - 1)


def swap(array, k):
    return lax.ppermute(array, "band", [(i, i ^ k) for i in range(16)])


def exchange(blocks):
    return lax.all_to_all(blocks, "band", 0, 0, tiled=True)


def start_all(copies):
    for copy in copies:
        copy.start()
    return copies


GATHER = 256


def gather_kernel(ids_hbm, grid_hbm, out_hbm, ids_ref, grid_ref, sel_ref, out_ref, sems):
    window, cap = ids_ref.shape[1:]
    ids_copy, grid_copy = start_all(
        [
            pltpu.make_async_copy(ids_hbm, ids_ref, sems.at[0]),
            pltpu.make_async_copy(grid_hbm, grid_ref, sems.at[1]),
        ]
    )
    d = lax.axis_index("band")
    lane = lax.broadcasted_iota(jnp.int32, (cap, window), 1)
    column = lax.broadcasted_iota(jnp.int32, (cap, grid_ref.shape[0]), 1)
    ids_copy.wait()
    table = jnp.transpose(ids_ref[0].astype(f32))
    rows = GATHER
    copies = []
    for i in range(out_ref.shape[0] // rows):
        part = slice(i * rows, (i + 1) * rows)
        for place in range(i * rows // cap, (i + 1) * rows // cap):
            mine = jnp.where(lane == slot_of(place, d, window), table, 0.0)
            ids = jnp.sum(mine, axis=1, keepdims=True).astype(jnp.int32)
            sel_ref[place * cap : (place + 1) * cap] = (ids == column).astype(f32).astype(bf16)
        if i == 0:
            grid_copy.wait()
        out_ref[part] = mm(sel_ref[part], grid_ref[...]).astype(bf16)
        copies += start_all([pltpu.make_async_copy(out_ref.at[part], out_hbm.at[part], sems.at[2 + i])])
    for copy in copies:
        copy.wait()


def gather(send_rows, grid_lat):
    window, cap = send_rows.shape[1:]
    shape = (window * cap, grid_lat.shape[1])
    return pl.pallas_call(
        gather_kernel,
        out_shape=jax.ShapeDtypeStruct(shape, bf16),
        in_specs=[HBM, HBM],
        out_specs=HBM,
        scratch_shapes=[
            pltpu.VMEM(send_rows.shape, jnp.int32),
            pltpu.VMEM(grid_lat.shape, bf16),
            pltpu.VMEM((shape[0], grid_lat.shape[0]), bf16),
            pltpu.VMEM(shape, bf16),
            pltpu.SemaphoreType.DMA((2 + shape[0] // GATHER,)),
        ],
        compiler_params=pltpu.CompilerParams(vmem_limit_bytes=VMEM),
        cost_estimate=QUICK,
        name="gather_rows",
    )(send_rows, grid_lat)


def own_kernel(
    edges_hbm, mesh_hbm, w1_hbm, out_hbm, pre_hbm,
    edges_ref, mesh_ref, w1_ref, out_ref, pre_ref, sem,
):
    width = edges_ref.shape[1]
    nodes = mesh_ref.shape[0]
    slots = edges_ref.shape[0] // nodes
    few = 16
    block = few * slots
    blocks = nodes // few
    loads = [
        pltpu.make_async_copy(
            edges_hbm.at[i * block : (i + 1) * block], edges_ref.at[i * block : (i + 1) * block], sem.at[i]
        )
        for i in range(blocks)
    ]
    loads += [
        pltpu.make_async_copy(mesh_hbm, mesh_ref, sem.at[blocks]),
        pltpu.make_async_copy(w1_hbm.at[:width], w1_ref.at[:width], sem.at[blocks + 1]),
        pltpu.make_async_copy(w1_hbm.at[2 * width :], w1_ref.at[width:], sem.at[blocks + 2]),
    ]
    start_all(loads)
    to = lax.broadcasted_iota(jnp.int32, (block, block), 0)
    at = lax.broadcasted_iota(jnp.int32, (block, block), 1)
    turn = (at == (to % few) * slots + to // few).astype(f32).astype(bf16)
    for i in range(blocks):
        loads[i].wait()
        rows = mm(turn, edges_ref[i * block : (i + 1) * block]).astype(bf16)
        for k in range(slots):
            out_ref[k * nodes + i * few : k * nodes + (i + 1) * few] = rows[k * few : (k + 1) * few]
    copies = start_all([pltpu.make_async_copy(out_ref, out_hbm, sem.at[0])])
    for copy in loads[blocks:]:
        copy.wait()
    for k in range(slots):
        part = slice(k * nodes, (k + 1) * nodes)
        both = jnp.concatenate([out_ref[part], mesh_ref[...]], axis=1)
        pre_ref[part] = mm(both, w1_ref[...])
        copies += start_all(
            [pltpu.make_async_copy(pre_ref.at[part], pre_hbm.at[part], sem.at[blocks + 3 + k])]
        )
    for copy in copies:
        copy.wait()


def own(edges, mesh_lat, w1):
    total, width = edges.shape
    sd = jax.ShapeDtypeStruct
    nodes = mesh_lat.shape[0]
    return pl.pallas_call(
        own_kernel,
        out_shape=[sd((total, width), bf16), sd((total, width), f32)],
        in_specs=[HBM] * 3,
        out_specs=[HBM] * 2,
        scratch_shapes=[
            pltpu.VMEM((total, width), bf16),
            pltpu.VMEM(mesh_lat.shape, bf16),
            pltpu.VMEM((2 * width, width), bf16),
            pltpu.VMEM((total, width), bf16),
            pltpu.VMEM((total, width), f32),
            pltpu.SemaphoreType.DMA((nodes // 16 + 3 + total // nodes,)),
        ],
        compiler_params=pltpu.CompilerParams(vmem_limit_bytes=VMEM),
        cost_estimate=QUICK,
        name="own_terms",
    )(edges, mesh_lat, w1)


def sigmoid(v):
    return 1.0 / (1.0 + jnp.exp(-v))


def row_mean(v):
    return jnp.mean(v, axis=-1, keepdims=True)


STEP = 512


def slot_places(src, window, cap):
    d = lax.axis_index("band")
    return ((d - src // cap + window // 2) & (window - 1)) * cap + (src & (cap - 1))


def middle_kernel(
    window, pre_hbm, arrived_hbm, w1_hbm, w2_hbm, mesh_hbm, cot_hbm, v1_hbm, n2_hbm,
    mask_hbm, src_hbm,
    new_hbm, gslot_hbm, gproj_hbm, g1_hbm,
    pre, arrived_ref, w1g_ref, w2_ref, mesh_ref, cot_ref, v1_ref, n2_ref, mask_ref,
    src_ref, new_ref, gslot_ref,
    proj, dsilu, hn, rm, agg, g1_ref, gproj_ref, sems,
):
    width = w2_ref.shape[0]
    nodes = mesh_ref.shape[0]
    total = pre_hbm.shape[0]
    steps = total // STEP
    per = STEP // nodes
    cap = arrived_ref.shape[0] // window
    small = [
        (w1_hbm.at[width : 2 * width], w1g_ref), (arrived_hbm, arrived_ref), (src_hbm, src_ref),
        (mask_hbm, mask_ref), (w2_hbm, w2_ref),
        (mesh_hbm, mesh_ref), (v1_hbm, v1_ref), (n2_hbm, n2_ref), (cot_hbm, cot_ref),
    ]
    small = [pltpu.make_async_copy(*pair, sems.at[i]) for i, pair in enumerate(small)]
    loads = []
    for i in range(steps):
        part = slice(i * STEP, (i + 1) * STEP)
        loads.append(pltpu.make_async_copy(pre_hbm.at[part], pre.at[part], sems.at[len(small) + i]))
    start_all(small[:2] + loads[:1] + small[2:5] + loads[1:] + small[5:])
    for copy in small[:2]:
        copy.wait()
    proj[...] = mm(arrived_ref[...], w1g_ref[...]).astype(bf16)
    for copy in small[2:5]:
        copy.wait()
    place = slot_places(src_ref[...], window, cap).astype(f32)
    both = jnp.transpose(jnp.concatenate([place, mask_ref[...].astype(f32)], axis=0))
    slots = place.shape[0]
    column = lax.broadcasted_iota(jnp.int32, (nodes, proj.shape[0]), 1)
    agg[...] = jnp.zeros_like(agg)
    for i in range(steps):
        part = slice(i * STEP, (i + 1) * STEP)
        hot = jnp.concatenate(
            [
                (both[:, k : k + 1].astype(jnp.int32) == column).astype(f32).astype(bf16)
                for k in range(i * per, (i + 1) * per)
            ],
            axis=0,
        )
        got = mm(hot, proj[...])
        loads[i].wait()
        v = pre[part] + got
        sig = sigmoid(v)
        hid = v * sig
        dsilu[part] = sig + hid * (1.0 - sig)
        p2 = mm(hid.astype(bf16), w2_ref[...])
        c = p2 - row_mean(p2)
        r = lax.rsqrt(row_mean(c * c) + eps)
        h = c * r
        hn[part] = h
        m = jnp.concatenate(
            [both[:, slots + k : slots + k + 1] for k in range(i * per, (i + 1) * per)], axis=0
        )
        rm[part] = r * m
        msg = h * m
        add = msg[:nodes]
        for n in range(1, per):
            add = add + msg[n * nodes : (n + 1) * nodes]
        agg[...] += add
    for copy in small[5:]:
        copy.wait()
    mesh = mesh_ref[...]
    p3 = mm(mesh, v1_ref[:width]) + mm(agg[...].astype(bf16), v1_ref[width:])
    sig = sigmoid(p3)
    a3 = p3 * sig
    p4 = mm(a3.astype(bf16), n2_ref[...])
    c = p4 - row_mean(p4)
    r = lax.rsqrt(row_mean(c * c) + eps)
    h = c * r
    new_ref[...] = (mesh.astype(f32) + h).astype(bf16)
    stores = start_all([pltpu.make_async_copy(new_ref, new_hbm, sems.at[0])])
    cot = cot_ref[...].astype(f32)
    g4 = (r * (cot - row_mean(cot) - h * row_mean(cot * h))).astype(bf16)
    g3 = (mm_t(g4, n2_ref[...]) * (sig + a3 * (1.0 - sig))).astype(bf16)
    ga = mm_t(g3, v1_ref[width:])
    agg[...] = ga - row_mean(ga)
    for i in range(steps):
        part = slice(i * STEP, (i + 1) * STEP)
        ga = jnp.concatenate([agg[...]] * per, axis=0)
        h = hn[part]
        g2 = rm[part] * (ga - h * row_mean(ga * h))
        g1_ref[part] = (mm_t(g2.astype(bf16), w2_ref[...]) * dsilu[part]).astype(bf16)
    stores += start_all([pltpu.make_async_copy(g1_ref, g1_hbm, sems.at[1])])
    src = slot_places(src_ref[...], window, cap)
    rows = 256
    for i in range(gproj_ref.shape[0] // rows):
        part = slice(i * rows, (i + 1) * rows)
        slot = lax.broadcasted_iota(jnp.int32, (rows, nodes), 0) + i * rows
        sel = jnp.concatenate(
            [(slot == src[k : k + 1]).astype(f32).astype(bf16) for k in range(slots)], axis=1
        )
        gp = mm(sel, g1_ref[...]).astype(bf16)
        gproj_ref[part] = gp
        gslot_ref[part] = mm_t(gp, w1g_ref[...]).astype(bf16)
        stores += start_all(
            [
                pltpu.make_async_copy(gslot_ref.at[part], gslot_hbm.at[part], sems.at[2 + i]),
                pltpu.make_async_copy(gproj_ref.at[part], gproj_hbm.at[part], sems.at[6 + i]),
            ]
        )
    for copy in stores:
        copy.wait()


SHARE = [4 * kz + 2 * ky for ky in range(2) for kz in (2, 3, 0, 1)]
PIECES = 4


def middle(window, pre, arrived, w1, w2, mesh_lat, cot, v1, n2, mask, src):
    total, width = pre.shape
    nodes = mesh_lat.shape[0]
    sd = jax.ShapeDtypeStruct
    vm = pltpu.VMEM
    return pl.pallas_call(
        functools.partial(middle_kernel, window),
        out_shape=[
            sd((nodes, width), bf16), sd(arrived.shape, bf16), sd(arrived.shape, bf16),
            sd((total, width), bf16),
        ],
        in_specs=[HBM] * 10,
        out_specs=[HBM] * 4,
        scratch_shapes=[
            vm((total, width), f32),
            vm(arrived.shape, bf16),
            vm(w2.shape, bf16),
            vm(w2.shape, bf16),
            vm(mesh_lat.shape, bf16),
            vm(cot.shape, bf16),
            vm(v1.shape, bf16),
            vm(n2.shape, bf16),
            vm(mask.shape, jnp.int32),
            vm(src.shape, jnp.int32),
            vm(mesh_lat.shape, bf16),
            vm(arrived.shape, bf16),
            vm(arrived.shape, bf16),
            vm((total, width), f32),
            vm((total, width), f32),
            vm((total, 1), f32),
            vm((nodes, width), f32),
            vm((total, width), bf16),
            vm(arrived.shape, bf16),
            pltpu.SemaphoreType.DMA((10 + total // STEP,)),
        ],
        compiler_params=pltpu.CompilerParams(vmem_limit_bytes=VMEM),
        cost_estimate=QUICK,
        name="edges_and_nodes",
    )(pre, arrived, w1, w2, mesh_lat, cot, v1, n2, mask, src)


def terms_kernel(edges_ref, g1_ref, mesh_ref, arrived_ref, gproj_ref, *rest):
    keep, send, term = rest[:PIECES], rest[PIECES:-1], rest[-1]
    width = g1_ref.shape[1]
    nodes = mesh_ref.shape[0]
    g1 = g1_ref[...]
    term[:width] = outer_sum(edges_ref[...], g1)
    term[width : 2 * width] = outer_sum(arrived_ref[...], gproj_ref[...])
    gsum = g1[:nodes].astype(f32)
    for k in range(1, g1.shape[0] // nodes):
        gsum = gsum + g1[k * nodes : (k + 1) * nodes].astype(f32)
    term[2 * width :] = outer_sum(mesh_ref[...], gsum.astype(bf16))
    share = keep[0].shape[1]
    d = lax.axis_index("band")
    for i, k in enumerate(SHARE):
        at = pl.ds(pl.multiple_of((d ^ k ^ 1) * share, share), share)
        send[i // 2][i % 2] = term[at].astype(bf16)
    for i, k in enumerate(SHARE):
        at = pl.ds(pl.multiple_of((d ^ k) * share, share), share)
        keep[i // 2][i % 2] = term[at]


def terms(edges, g1, mesh_lat, arrived, gproj):
    width = g1.shape[1]
    share = (2, 3 * width // 16, width)
    sd = jax.ShapeDtypeStruct
    out = pl.pallas_call(
        terms_kernel,
        out_shape=[sd(share, f32)] * PIECES + [sd(share, bf16)] * PIECES,
        in_specs=[VM] * 5,
        out_specs=[VM] * (2 * PIECES),
        scratch_shapes=[pltpu.VMEM((3 * width, width), f32)],
        compiler_params=pltpu.CompilerParams(vmem_limit_bytes=16 << 20),
        cost_estimate=QUICK,
        name="w1_terms",
    )(edges, g1, mesh_lat, arrived, gproj)
    return out[:PIECES], out[PIECES:]


def share_sum(keep, send):
    full = [mine + swap(other, 1).astype(f32) for mine, other in zip(keep, send)]
    half = len(full) // 2
    full = [mine + swap(other.astype(bf16), 2).astype(f32) for mine, other in zip(full, full[half:])]
    far, near = full
    others = [swap(far[0].astype(bf16), 8), swap(far[1].astype(bf16), 12), swap(near[1].astype(bf16), 4)]
    return near[0], others


def grid_kernel(ids_ref, rows_ref, out_hbm, at_ref, out_ref, sems):
    window, cap = ids_ref.shape[1:]
    d = lax.axis_index("band")
    for place in range(window):
        at_ref[:, place * cap : (place + 1) * cap] = ids_ref[0, pl.ds(slot_of(place, d, window), 1), :]
    ids = at_ref[...]
    block = 256
    copies = []
    for i in range(out_ref.shape[0] // block):
        part = slice(i * block, (i + 1) * block)
        row = lax.broadcasted_iota(jnp.int32, (block, ids.shape[1]), 0) + i * block
        sel = (row == ids).astype(f32).astype(bf16)
        out_ref[part] = mm(sel, rows_ref[...]).astype(bf16)
        copies += start_all([pltpu.make_async_copy(out_ref.at[part], out_hbm.at[part], sems.at[i])])
    for copy in copies:
        copy.wait()


def grid_sum(send_rows, rows, grid_rows):
    slots, width = rows.shape
    return pl.pallas_call(
        grid_kernel,
        out_shape=jax.ShapeDtypeStruct((grid_rows, width), bf16),
        in_specs=[VM] * 2,
        out_specs=HBM,
        scratch_shapes=[
            pltpu.VMEM((1, slots), jnp.int32),
            pltpu.VMEM((grid_rows, width), bf16),
            pltpu.SemaphoreType.DMA((grid_rows // 256,)),
        ],
        compiler_params=pltpu.CompilerParams(vmem_limit_bytes=10 << 20),
        cost_estimate=pl.CostEstimate(
            flops=2 * grid_rows * slots * width, bytes_accessed=4 << 20, transcendentals=0
        ),
        name="grid_sum",
    )(send_rows, rows)


def per_device_all(
    grid_lat, mesh_lat, edge_lat, edge_w1, edge_w2, node_w1, node_w2, mesh_cot,
    send_rows, edge_src, edge_mask,
):
    width = mesh_lat.shape[1]
    nodes, slots = edge_src.shape
    arrived = exchange(gather(send_rows, grid_lat))

    edges, pre = own(edge_lat.reshape(nodes * slots, width), mesh_lat, edge_w1)
    src = jnp.transpose(edge_src)
    mask = jnp.transpose(edge_mask)

    mesh_new, gslot, gproj, g1 = middle(
        send_rows.shape[1], pre, arrived, edge_w1, edge_w2, mesh_lat, mesh_cot, node_w1,
        node_w2, mask, src,
    )
    returned = exchange(gslot)
    keep, send = terms(edges, g1, mesh_lat, arrived, gproj)
    mine, others = share_sum(keep, send)
    grid_grad = grid_sum(send_rows, returned, grid_lat.shape[0])
    grid_grad, w1_grad = lax.optimization_barrier((grid_grad, mine))
    for other in others:
        w1_grad = w1_grad + other.astype(f32)
    return (mesh_new, grid_grad, w1_grad)


def solution(mesh):
    in_specs = (
        P(("group", "band"), None),
        P(("group", "band"), None),
        P(("group", "band"), None, None),
        P(),
        P(),
        P(),
        P(),
        P(("group", "band"), None),
        P("band", None, None),
        P("band", None),
        P("band", None),
    )
    out_specs = (P(("group", "band"), None), P(("group", "band"), None), P(("group", "band"), None))

    def step(*args):
        window = args[8].shape[1]
        every = mesh.shape["band"] == window == 16
        body = per_device_all if every else per_device_window
        return jax.shard_map(
            body, mesh=mesh, in_specs=in_specs, out_specs=out_specs, check_vma=False
        )(*args)

    return step
```

```python
import functools

import jax
import jax.numpy as jnp
from jax import lax
from jax.experimental import pallas as pl
from jax.experimental.pallas import tpu as pltpu
from jax.sharding import PartitionSpec as P

eps = 1e-05
f32 = jnp.float32
bf16 = jnp.bfloat16
VM = pl.BlockSpec(memory_space=pltpu.VMEM)
HBM = pl.BlockSpec(memory_space=pltpu.HBM)
VMEM = 63 << 20
QUICK = pl.CostEstimate(flops=1, bytes_accessed=1, transcendentals=0)


def from_behind(array, axis, by):
    devices = lax.axis_size(axis)
    return lax.ppermute(array, axis, [(i, (i + by) % devices) for i in range(devices)])


def layer_norm(value):
    centred = value - jnp.mean(value, axis=-1, keepdims=True)
    scale = lax.rsqrt(jnp.mean(centred * centred, axis=-1, keepdims=True) + eps)
    return centred * scale


def norm_back(value, grad):
    centred = value - jnp.mean(value, axis=-1, keepdims=True)
    scale = lax.rsqrt(jnp.mean(centred * centred, axis=-1, keepdims=True) + eps)
    normed = centred * scale
    return scale * (
        grad
        - jnp.mean(grad, axis=-1, keepdims=True)
        - normed * jnp.mean(grad * normed, axis=-1, keepdims=True)
    )


def silu_grad(value):
    sig = jax.nn.sigmoid(value)
    return sig * (1.0 + value * (1.0 - sig))


def outer_sum(left, right):
    return lax.dot_general(
        left, right, (((0,), (0,)), ((), ())), preferred_element_type=f32
    )


def mm(left, right):
    return jnp.dot(left, right, preferred_element_type=f32)


def mm_t(left, right):
    return lax.dot_general(
        left, right, (((1,), (1,)), ((), ())), preferred_element_type=f32
    )


def send_forward(outgoing):
    window = outgoing.shape[0]
    half = window // 2
    pieces = []
    for slot in range(window):
        offset = slot - half
        if offset == 0:
            pieces.append(outgoing[slot])
        else:
            pieces.append(from_behind(outgoing[slot], "band", offset))
    return jnp.stack(pieces, axis=0)


def return_rows(grads):
    window = grads.shape[0]
    half = window // 2
    pieces = []
    for slot in range(window):
        offset = slot - half
        if offset == 0:
            pieces.append(grads[slot])
        else:
            pieces.append(
                from_behind(grads[slot].astype(bf16), "band", -offset).astype(f32)
            )
    return jnp.stack(pieces, axis=0)


def per_device_window(
    grid_lat, mesh_lat, edge_lat, edge_w1, edge_w2, node_w1, node_w2, mesh_cot,
    send_rows, edge_src, edge_mask,
):
    width = mesh_lat.shape[1]
    nodes, slots = edge_src.shape
    window = send_rows.shape[1]
    cap = send_rows.shape[2]
    w1e = edge_w1[:width]
    w1g = edge_w1[width : 2 * width]
    w1m = edge_w1[2 * width :]
    v1m = node_w1[:width]
    v1a = node_w1[width:]
    row_ids = send_rows[0].reshape(-1)
    outgoing_raw = grid_lat[row_ids]
    arrived = send_forward(outgoing_raw.reshape(window, cap, width)).reshape(window * cap, width)
    proj = mm(arrived, w1g).astype(bf16)
    flat_src = edge_src.reshape(-1)
    edges = edge_lat.reshape(nodes * slots, width)
    mesh_rep = jnp.repeat(mesh_lat, slots, axis=0)
    maskf = edge_mask.reshape(-1, 1).astype(f32)
    pre1 = mm(edges, w1e) + mm(mesh_rep, w1m) + proj[flat_src].astype(f32)
    hid = jax.nn.silu(pre1).astype(bf16)
    pre2 = mm(hid, edge_w2)
    msg = layer_norm(pre2) * maskf
    agg = jnp.sum(msg.reshape(nodes, slots, width), axis=1).astype(bf16)
    pre3 = mm(mesh_lat, v1m) + mm(agg, v1a)
    act = jax.nn.silu(pre3).astype(bf16)
    pre4 = mm(act, node_w2)
    mesh_new = (mesh_lat.astype(f32) + layer_norm(pre4)).astype(bf16)
    g4 = norm_back(pre4, mesh_cot.astype(f32)).astype(bf16)
    g3 = (mm(g4, node_w2.T) * silu_grad(pre3)).astype(bf16)
    gagg = mm(g3, v1a.T)
    g2 = norm_back(pre2, jnp.repeat(gagg, slots, axis=0) * maskf).astype(bf16)
    g1 = (mm(g2, edge_w2.T) * silu_grad(pre1)).astype(bf16)
    gproj = jnp.zeros((window * cap, width), f32).at[flat_src].add(g1.astype(f32)).astype(bf16)
    term_e = outer_sum(edges, g1)
    term_m = outer_sum(mesh_rep, g1)
    term_g = outer_sum(arrived, gproj)
    local_slot = mm(gproj, w1g.T)
    gslot = return_rows(local_slot.reshape(window, cap, width)).reshape(window * cap, width)
    grid_grad = jnp.zeros((grid_lat.shape[0], width), f32).at[row_ids].add(gslot).astype(bf16)
    term = jnp.concatenate([term_e, term_g, term_m], axis=0)
    w1_grad = lax.psum_scatter(term, "band", scatter_dimension=0, tiled=True)
    return (mesh_new, grid_grad, w1_grad)


def slot_of(place, d, window):
    return (place - d + window // 2) & (window - 1)


def swap(array, k):
    return lax.ppermute(array, "band", [(i, i ^ k) for i in range(16)])


def exchange(blocks):
    return lax.all_to_all(blocks, "band", 0, 0, tiled=True)


def start_all(copies):
    for copy in copies:
        copy.start()
    return copies


GATHER = 256


def gather_kernel(ids_hbm, grid_hbm, out_hbm, ids_ref, grid_ref, sel_ref, out_ref, sems):
    window, cap = ids_ref.shape[1:]
    ids_copy, grid_copy = start_all(
        [
            pltpu.make_async_copy(ids_hbm, ids_ref, sems.at[0]),
            pltpu.make_async_copy(grid_hbm, grid_ref, sems.at[1]),
        ]
    )
    d = lax.axis_index("band")
    lane = lax.broadcasted_iota(jnp.int32, (cap, window), 1)
    column = lax.broadcasted_iota(jnp.int32, (cap, grid_ref.shape[0]), 1)
    ids_copy.wait()
    table = jnp.transpose(ids_ref[0].astype(f32))
    rows = GATHER
    copies = []
    for i in range(out_ref.shape[0] // rows):
        part = slice(i * rows, (i + 1) * rows)
        for place in range(i * rows // cap, (i + 1) * rows // cap):
            mine = jnp.where(lane == slot_of(place, d, window), table, 0.0)
            ids = jnp.sum(mine, axis=1, keepdims=True).astype(jnp.int32)
            sel_ref[place * cap : (place + 1) * cap] = (ids == column).astype(f32).astype(bf16)
        if i == 0:
            grid_copy.wait()
        out_ref[part] = mm(sel_ref[part], grid_ref[...]).astype(bf16)
        copies += start_all([pltpu.make_async_copy(out_ref.at[part], out_hbm.at[part], sems.at[2 + i])])
    for copy in copies:
        copy.wait()


def gather(send_rows, grid_lat):
    window, cap = send_rows.shape[1:]
    shape = (window * cap, grid_lat.shape[1])
    return pl.pallas_call(
        gather_kernel,
        out_shape=jax.ShapeDtypeStruct(shape, bf16),
        in_specs=[HBM, HBM],
        out_specs=HBM,
        scratch_shapes=[
            pltpu.VMEM(send_rows.shape, jnp.int32),
            pltpu.VMEM(grid_lat.shape, bf16),
            pltpu.VMEM((shape[0], grid_lat.shape[0]), bf16),
            pltpu.VMEM(shape, bf16),
            pltpu.SemaphoreType.DMA((2 + shape[0] // GATHER,)),
        ],
        compiler_params=pltpu.CompilerParams(vmem_limit_bytes=VMEM),
        cost_estimate=QUICK,
        name="gather_rows",
    )(send_rows, grid_lat)


def own_kernel(
    edges_hbm, mesh_hbm, w1_hbm, out_hbm, pre_hbm,
    edges_ref, mesh_ref, w1_ref, out_ref, pre_ref, sem,
):
    width = edges_ref.shape[1]
    nodes = mesh_ref.shape[0]
    slots = edges_ref.shape[0] // nodes
    few = 16
    block = few * slots
    blocks = nodes // few
    loads = [
        pltpu.make_async_copy(
            edges_hbm.at[i * block : (i + 1) * block], edges_ref.at[i * block : (i + 1) * block], sem.at[i]
        )
        for i in range(blocks)
    ]
    loads += [
        pltpu.make_async_copy(mesh_hbm, mesh_ref, sem.at[blocks]),
        pltpu.make_async_copy(w1_hbm.at[:width], w1_ref.at[:width], sem.at[blocks + 1]),
        pltpu.make_async_copy(w1_hbm.at[2 * width :], w1_ref.at[width:], sem.at[blocks + 2]),
    ]
    start_all(loads)
    to = lax.broadcasted_iota(jnp.int32, (block, block), 0)
    at = lax.broadcasted_iota(jnp.int32, (block, block), 1)
    turn = (at == (to % few) * slots + to // few).astype(f32).astype(bf16)
    for i in range(blocks):
        loads[i].wait()
        rows = mm(turn, edges_ref[i * block : (i + 1) * block]).astype(bf16)
        for k in range(slots):
            out_ref[k * nodes + i * few : k * nodes + (i + 1) * few] = rows[k * few : (k + 1) * few]
    copies = start_all([pltpu.make_async_copy(out_ref, out_hbm, sem.at[0])])
    for copy in loads[blocks:]:
        copy.wait()
    for k in range(slots):
        part = slice(k * nodes, (k + 1) * nodes)
        both = jnp.concatenate([out_ref[part], mesh_ref[...]], axis=1)
        pre_ref[part] = mm(both, w1_ref[...])
        copies += start_all(
            [pltpu.make_async_copy(pre_ref.at[part], pre_hbm.at[part], sem.at[blocks + 3 + k])]
        )
    for copy in copies:
        copy.wait()


def own(edges, mesh_lat, w1):
    total, width = edges.shape
    sd = jax.ShapeDtypeStruct
    nodes = mesh_lat.shape[0]
    return pl.pallas_call(
        own_kernel,
        out_shape=[sd((total, width), bf16), sd((total, width), f32)],
        in_specs=[HBM] * 3,
        out_specs=[HBM] * 2,
        scratch_shapes=[
            pltpu.VMEM((total, width), bf16),
            pltpu.VMEM(mesh_lat.shape, bf16),
            pltpu.VMEM((2 * width, width), bf16),
            pltpu.VMEM((total, width), bf16),
            pltpu.VMEM((total, width), f32),
            pltpu.SemaphoreType.DMA((nodes // 16 + 3 + total // nodes,)),
        ],
        compiler_params=pltpu.CompilerParams(vmem_limit_bytes=VMEM),
        cost_estimate=QUICK,
        name="own_terms",
    )(edges, mesh_lat, w1)


def sigmoid(v):
    return 1.0 / (1.0 + jnp.exp(-v))


def row_mean(v):
    return jnp.mean(v, axis=-1, keepdims=True)


STEP = 512


def slot_places(src, window, cap):
    d = lax.axis_index("band")
    return ((d - src // cap + window // 2) & (window - 1)) * cap + (src & (cap - 1))


def middle_kernel(
    window, pre_hbm, arrived_hbm, w1_hbm, w2_hbm, mesh_hbm, cot_hbm, v1_hbm, n2_hbm,
    mask_hbm, src_hbm,
    new_hbm, gslot_hbm, gproj_hbm, g1_hbm,
    pre, arrived_ref, w1g_ref, w2_ref, mesh_ref, cot_ref, v1_ref, n2_ref, mask_ref,
    src_ref, new_ref, gslot_ref,
    proj, dsilu, hn, rm, agg, g1_ref, gproj_ref, sems,
):
    width = w2_ref.shape[0]
    nodes = mesh_ref.shape[0]
    total = pre_hbm.shape[0]
    steps = total // STEP
    per = STEP // nodes
    cap = arrived_ref.shape[0] // window
    small = [
        (w1_hbm.at[width : 2 * width], w1g_ref), (arrived_hbm, arrived_ref), (src_hbm, src_ref),
        (mask_hbm, mask_ref), (w2_hbm, w2_ref),
        (mesh_hbm, mesh_ref), (v1_hbm, v1_ref), (n2_hbm, n2_ref), (cot_hbm, cot_ref),
    ]
    small = [pltpu.make_async_copy(*pair, sems.at[i]) for i, pair in enumerate(small)]
    loads = []
    for i in range(steps):
        part = slice(i * STEP, (i + 1) * STEP)
        loads.append(pltpu.make_async_copy(pre_hbm.at[part], pre.at[part], sems.at[len(small) + i]))
    start_all(small[:2] + loads[:1] + small[2:5] + loads[1:] + small[5:])
    for copy in small[:2]:
        copy.wait()
    proj[...] = mm(arrived_ref[...], w1g_ref[...]).astype(bf16)
    for copy in small[2:5]:
        copy.wait()
    place = slot_places(src_ref[...], window, cap).astype(f32)
    both = jnp.transpose(jnp.concatenate([place, mask_ref[...].astype(f32)], axis=0))
    slots = place.shape[0]
    column = lax.broadcasted_iota(jnp.int32, (nodes, proj.shape[0]), 1)
    agg[...] = jnp.zeros_like(agg)
    for i in range(steps):
        part = slice(i * STEP, (i + 1) * STEP)
        hot = jnp.concatenate(
            [
                (both[:, k : k + 1].astype(jnp.int32) == column).astype(f32).astype(bf16)
                for k in range(i * per, (i + 1) * per)
            ],
            axis=0,
        )
        got = mm(hot, proj[...])
        loads[i].wait()
        v = pre[part] + got
        sig = sigmoid(v)
        hid = v * sig
        dsilu[part] = sig + hid * (1.0 - sig)
        p2 = mm(hid.astype(bf16), w2_ref[...])
        c = p2 - row_mean(p2)
        r = lax.rsqrt(row_mean(c * c) + eps)
        h = c * r
        hn[part] = h
        m = jnp.concatenate(
            [both[:, slots + k : slots + k + 1] for k in range(i * per, (i + 1) * per)], axis=0
        )
        rm[part] = r * m
        msg = h * m
        add = msg[:nodes]
        for n in range(1, per):
            add = add + msg[n * nodes : (n + 1) * nodes]
        agg[...] += add
    for copy in small[5:]:
        copy.wait()
    mesh = mesh_ref[...]
    p3 = mm(mesh, v1_ref[:width]) + mm(agg[...].astype(bf16), v1_ref[width:])
    sig = sigmoid(p3)
    a3 = p3 * sig
    p4 = mm(a3.astype(bf16), n2_ref[...])
    c = p4 - row_mean(p4)
    r = lax.rsqrt(row_mean(c * c) + eps)
    h = c * r
    new_ref[...] = (mesh.astype(f32) + h).astype(bf16)
    stores = start_all([pltpu.make_async_copy(new_ref, new_hbm, sems.at[0])])
    cot = cot_ref[...].astype(f32)
    g4 = (r * (cot - row_mean(cot) - h * row_mean(cot * h))).astype(bf16)
    g3 = (mm_t(g4, n2_ref[...]) * (sig + a3 * (1.0 - sig))).astype(bf16)
    ga = mm_t(g3, v1_ref[width:])
    agg[...] = ga - row_mean(ga)
    wide = 2 * STEP
    for i in range(total // wide):
        part = slice(i * wide, (i + 1) * wide)
        ga = jnp.concatenate([agg[...]] * (wide // nodes), axis=0)
        h = hn[part]
        g2 = rm[part] * (ga - h * row_mean(ga * h))
        g1_ref[part] = (mm_t(g2.astype(bf16), w2_ref[...]) * dsilu[part]).astype(bf16)
    stores += start_all([pltpu.make_async_copy(g1_ref, g1_hbm, sems.at[1])])
    src = slot_places(src_ref[...], window, cap)
    rows = 512
    for i in range(gproj_ref.shape[0] // rows):
        part = slice(i * rows, (i + 1) * rows)
        slot = lax.broadcasted_iota(jnp.int32, (rows, nodes), 0) + i * rows
        sel = jnp.concatenate(
            [(slot == src[k : k + 1]).astype(f32).astype(bf16) for k in range(slots)], axis=1
        )
        gp = mm(sel, g1_ref[...]).astype(bf16)
        gproj_ref[part] = gp
        gslot_ref[part] = mm_t(gp, w1g_ref[...]).astype(bf16)
        stores += start_all(
            [
                pltpu.make_async_copy(gslot_ref.at[part], gslot_hbm.at[part], sems.at[2 + i]),
                pltpu.make_async_copy(gproj_ref.at[part], gproj_hbm.at[part], sems.at[6 + i]),
            ]
        )
    for copy in stores:
        copy.wait()


SHARE = [4 * kz + 2 * ky for ky in range(2) for kz in (2, 3, 0, 1)]
PIECES = 4


def middle(window, pre, arrived, w1, w2, mesh_lat, cot, v1, n2, mask, src):
    total, width = pre.shape
    nodes = mesh_lat.shape[0]
    sd = jax.ShapeDtypeStruct
    vm = pltpu.VMEM
    return pl.pallas_call(
        functools.partial(middle_kernel, window),
        out_shape=[
            sd((nodes, width), bf16), sd(arrived.shape, bf16), sd(arrived.shape, bf16),
            sd((total, width), bf16),
        ],
        in_specs=[HBM] * 10,
        out_specs=[HBM] * 4,
        scratch_shapes=[
            vm((total, width), f32),
            vm(arrived.shape, bf16),
            vm(w2.shape, bf16),
            vm(w2.shape, bf16),
            vm(mesh_lat.shape, bf16),
            vm(cot.shape, bf16),
            vm(v1.shape, bf16),
            vm(n2.shape, bf16),
            vm(mask.shape, jnp.int32),
            vm(src.shape, jnp.int32),
            vm(mesh_lat.shape, bf16),
            vm(arrived.shape, bf16),
            vm(arrived.shape, bf16),
            vm((total, width), f32),
            vm((total, width), f32),
            vm((total, 1), f32),
            vm((nodes, width), f32),
            vm((total, width), bf16),
            vm(arrived.shape, bf16),
            pltpu.SemaphoreType.DMA((10 + total // STEP,)),
        ],
        compiler_params=pltpu.CompilerParams(vmem_limit_bytes=VMEM),
        cost_estimate=QUICK,
        name="edges_and_nodes",
    )(pre, arrived, w1, w2, mesh_lat, cot, v1, n2, mask, src)


def terms_kernel(edges_ref, g1_ref, mesh_ref, arrived_ref, gproj_ref, *rest):
    keep, send, term = rest[:PIECES], rest[PIECES:-1], rest[-1]
    width = g1_ref.shape[1]
    nodes = mesh_ref.shape[0]
    g1 = g1_ref[...]
    term[:width] = outer_sum(edges_ref[...], g1)
    term[width : 2 * width] = outer_sum(arrived_ref[...], gproj_ref[...])
    gsum = g1[:nodes].astype(f32)
    for k in range(1, g1.shape[0] // nodes):
        gsum = gsum + g1[k * nodes : (k + 1) * nodes].astype(f32)
    term[2 * width :] = outer_sum(mesh_ref[...], gsum.astype(bf16))
    share = keep[0].shape[1]
    d = lax.axis_index("band")
    for i, k in enumerate(SHARE):
        at = pl.ds(pl.multiple_of((d ^ k ^ 1) * share, share), share)
        send[i // 2][i % 2] = term[at].astype(bf16)
    for i, k in enumerate(SHARE):
        at = pl.ds(pl.multiple_of((d ^ k) * share, share), share)
        keep[i // 2][i % 2] = term[at]


def terms(edges, g1, mesh_lat, arrived, gproj):
    width = g1.shape[1]
    share = (2, 3 * width // 16, width)
    sd = jax.ShapeDtypeStruct
    out = pl.pallas_call(
        terms_kernel,
        out_shape=[sd(share, f32)] * PIECES + [sd(share, bf16)] * PIECES,
        in_specs=[VM] * 5,
        out_specs=[VM] * (2 * PIECES),
        scratch_shapes=[pltpu.VMEM((3 * width, width), f32)],
        compiler_params=pltpu.CompilerParams(vmem_limit_bytes=16 << 20),
        cost_estimate=QUICK,
        name="w1_terms",
    )(edges, g1, mesh_lat, arrived, gproj)
    return out[:PIECES], out[PIECES:]


def share_sum(keep, send):
    full = [mine + swap(other, 1).astype(f32) for mine, other in zip(keep, send)]
    half = len(full) // 2
    full = [mine + swap(other.astype(bf16), 2).astype(f32) for mine, other in zip(full, full[half:])]
    far, near = full
    others = [swap(far[0].astype(bf16), 8), swap(far[1].astype(bf16), 12), swap(near[1].astype(bf16), 4)]
    return near[0], others


def grid_kernel(ids_ref, rows_ref, out_hbm, at_ref, out_ref, sems):
    window, cap = ids_ref.shape[1:]
    d = lax.axis_index("band")
    for place in range(window):
        at_ref[:, place * cap : (place + 1) * cap] = ids_ref[0, pl.ds(slot_of(place, d, window), 1), :]
    ids = at_ref[...]
    block = 256
    copies = []
    for i in range(out_ref.shape[0] // block):
        part = slice(i * block, (i + 1) * block)
        row = lax.broadcasted_iota(jnp.int32, (block, ids.shape[1]), 0) + i * block
        sel = (row == ids).astype(f32).astype(bf16)
        out_ref[part] = mm(sel, rows_ref[...]).astype(bf16)
        copies += start_all([pltpu.make_async_copy(out_ref.at[part], out_hbm.at[part], sems.at[i])])
    for copy in copies:
        copy.wait()


def grid_sum(send_rows, rows, grid_rows):
    slots, width = rows.shape
    return pl.pallas_call(
        grid_kernel,
        out_shape=jax.ShapeDtypeStruct((grid_rows, width), bf16),
        in_specs=[VM] * 2,
        out_specs=HBM,
        scratch_shapes=[
            pltpu.VMEM((1, slots), jnp.int32),
            pltpu.VMEM((grid_rows, width), bf16),
            pltpu.SemaphoreType.DMA((grid_rows // 256,)),
        ],
        compiler_params=pltpu.CompilerParams(vmem_limit_bytes=10 << 20),
        cost_estimate=pl.CostEstimate(
            flops=2 * grid_rows * slots * width, bytes_accessed=4 << 20, transcendentals=0
        ),
        name="grid_sum",
    )(send_rows, rows)


def per_device_all(
    grid_lat, mesh_lat, edge_lat, edge_w1, edge_w2, node_w1, node_w2, mesh_cot,
    send_rows, edge_src, edge_mask,
):
    width = mesh_lat.shape[1]
    nodes, slots = edge_src.shape
    arrived = exchange(gather(send_rows, grid_lat))

    edges, pre = own(edge_lat.reshape(nodes * slots, width), mesh_lat, edge_w1)
    src = jnp.transpose(edge_src)
    mask = jnp.transpose(edge_mask)

    mesh_new, gslot, gproj, g1 = middle(
        send_rows.shape[1], pre, arrived, edge_w1, edge_w2, mesh_lat, mesh_cot, node_w1,
        node_w2, mask, src,
    )
    returned = exchange(gslot)
    keep, send = terms(edges, g1, mesh_lat, arrived, gproj)
    mine, others = share_sum(keep, send)
    grid_grad = grid_sum(send_rows, returned, grid_lat.shape[0])
    grid_grad, w1_grad = lax.optimization_barrier((grid_grad, mine))
    for other in others:
        w1_grad = w1_grad + other.astype(f32)
    return (mesh_new, grid_grad, w1_grad)


def solution(mesh):
    in_specs = (
        P(("group", "band"), None),
        P(("group", "band"), None),
        P(("group", "band"), None, None),
        P(),
        P(),
        P(),
        P(),
        P(("group", "band"), None),
        P("band", None, None),
        P("band", None),
        P("band", None),
    )
    out_specs = (P(("group", "band"), None), P(("group", "band"), None), P(("group", "band"), None))

    def step(*args):
        window = args[8].shape[1]
        every = mesh.shape["band"] == window == 16
        body = per_device_all if every else per_device_window
        return jax.shard_map(
            body, mesh=mesh, in_specs=in_specs, out_specs=out_specs, check_vma=False
        )(*args)

    return step
```

```python
import functools

import jax
import jax.numpy as jnp
from jax import lax
from jax.experimental import pallas as pl
from jax.experimental.pallas import tpu as pltpu
from jax.sharding import PartitionSpec as P

eps = 1e-05
f32 = jnp.float32
bf16 = jnp.bfloat16
VM = pl.BlockSpec(memory_space=pltpu.VMEM)
HBM = pl.BlockSpec(memory_space=pltpu.HBM)
VMEM = 63 << 20
QUICK = pl.CostEstimate(flops=1, bytes_accessed=1, transcendentals=0)


def from_behind(array, axis, by):
    devices = lax.axis_size(axis)
    return lax.ppermute(array, axis, [(i, (i + by) % devices) for i in range(devices)])


def layer_norm(value):
    centred = value - jnp.mean(value, axis=-1, keepdims=True)
    scale = lax.rsqrt(jnp.mean(centred * centred, axis=-1, keepdims=True) + eps)
    return centred * scale


def norm_back(value, grad):
    centred = value - jnp.mean(value, axis=-1, keepdims=True)
    scale = lax.rsqrt(jnp.mean(centred * centred, axis=-1, keepdims=True) + eps)
    normed = centred * scale
    return scale * (
        grad
        - jnp.mean(grad, axis=-1, keepdims=True)
        - normed * jnp.mean(grad * normed, axis=-1, keepdims=True)
    )


def silu_grad(value):
    sig = jax.nn.sigmoid(value)
    return sig * (1.0 + value * (1.0 - sig))


def outer_sum(left, right):
    return lax.dot_general(
        left, right, (((0,), (0,)), ((), ())), preferred_element_type=f32
    )


def mm(left, right):
    return jnp.dot(left, right, preferred_element_type=f32)


def mm_t(left, right):
    return lax.dot_general(
        left, right, (((1,), (1,)), ((), ())), preferred_element_type=f32
    )


def send_forward(outgoing):
    window = outgoing.shape[0]
    half = window // 2
    pieces = []
    for slot in range(window):
        offset = slot - half
        if offset == 0:
            pieces.append(outgoing[slot])
        else:
            pieces.append(from_behind(outgoing[slot], "band", offset))
    return jnp.stack(pieces, axis=0)


def return_rows(grads):
    window = grads.shape[0]
    half = window // 2
    pieces = []
    for slot in range(window):
        offset = slot - half
        if offset == 0:
            pieces.append(grads[slot])
        else:
            pieces.append(
                from_behind(grads[slot].astype(bf16), "band", -offset).astype(f32)
            )
    return jnp.stack(pieces, axis=0)


def per_device_window(
    grid_lat, mesh_lat, edge_lat, edge_w1, edge_w2, node_w1, node_w2, mesh_cot,
    send_rows, edge_src, edge_mask,
):
    width = mesh_lat.shape[1]
    nodes, slots = edge_src.shape
    window = send_rows.shape[1]
    cap = send_rows.shape[2]
    w1e = edge_w1[:width]
    w1g = edge_w1[width : 2 * width]
    w1m = edge_w1[2 * width :]
    v1m = node_w1[:width]
    v1a = node_w1[width:]
    row_ids = send_rows[0].reshape(-1)
    outgoing_raw = grid_lat[row_ids]
    arrived = send_forward(outgoing_raw.reshape(window, cap, width)).reshape(window * cap, width)
    proj = mm(arrived, w1g).astype(bf16)
    flat_src = edge_src.reshape(-1)
    edges = edge_lat.reshape(nodes * slots, width)
    mesh_rep = jnp.repeat(mesh_lat, slots, axis=0)
    maskf = edge_mask.reshape(-1, 1).astype(f32)
    pre1 = mm(edges, w1e) + mm(mesh_rep, w1m) + proj[flat_src].astype(f32)
    hid = jax.nn.silu(pre1).astype(bf16)
    pre2 = mm(hid, edge_w2)
    msg = layer_norm(pre2) * maskf
    agg = jnp.sum(msg.reshape(nodes, slots, width), axis=1).astype(bf16)
    pre3 = mm(mesh_lat, v1m) + mm(agg, v1a)
    act = jax.nn.silu(pre3).astype(bf16)
    pre4 = mm(act, node_w2)
    mesh_new = (mesh_lat.astype(f32) + layer_norm(pre4)).astype(bf16)
    g4 = norm_back(pre4, mesh_cot.astype(f32)).astype(bf16)
    g3 = (mm(g4, node_w2.T) * silu_grad(pre3)).astype(bf16)
    gagg = mm(g3, v1a.T)
    g2 = norm_back(pre2, jnp.repeat(gagg, slots, axis=0) * maskf).astype(bf16)
    g1 = (mm(g2, edge_w2.T) * silu_grad(pre1)).astype(bf16)
    gproj = jnp.zeros((window * cap, width), f32).at[flat_src].add(g1.astype(f32)).astype(bf16)
    term_e = outer_sum(edges, g1)
    term_m = outer_sum(mesh_rep, g1)
    term_g = outer_sum(arrived, gproj)
    local_slot = mm(gproj, w1g.T)
    gslot = return_rows(local_slot.reshape(window, cap, width)).reshape(window * cap, width)
    grid_grad = jnp.zeros((grid_lat.shape[0], width), f32).at[row_ids].add(gslot).astype(bf16)
    term = jnp.concatenate([term_e, term_g, term_m], axis=0)
    w1_grad = lax.psum_scatter(term, "band", scatter_dimension=0, tiled=True)
    return (mesh_new, grid_grad, w1_grad)


def slot_of(place, d, window):
    return (place - d + window // 2) & (window - 1)


def swap(array, k):
    return lax.ppermute(array, "band", [(i, i ^ k) for i in range(16)])


def exchange(blocks):
    return lax.all_to_all(blocks, "band", 0, 0, tiled=True)


def start_all(copies):
    for copy in copies:
        copy.start()
    return copies


GATHER = 256


def gather_kernel(ids_hbm, grid_hbm, out_hbm, ids_ref, grid_ref, sel_ref, out_ref, sems):
    window, cap = ids_ref.shape[1:]
    ids_copy, grid_copy = start_all(
        [
            pltpu.make_async_copy(ids_hbm, ids_ref, sems.at[0]),
            pltpu.make_async_copy(grid_hbm, grid_ref, sems.at[1]),
        ]
    )
    d = lax.axis_index("band")
    lane = lax.broadcasted_iota(jnp.int32, (cap, window), 1)
    column = lax.broadcasted_iota(jnp.int32, (cap, grid_ref.shape[0]), 1)
    ids_copy.wait()
    table = jnp.transpose(ids_ref[0].astype(f32))
    rows = GATHER
    copies = []
    for i in range(out_ref.shape[0] // rows):
        part = slice(i * rows, (i + 1) * rows)
        for place in range(i * rows // cap, (i + 1) * rows // cap):
            mine = jnp.where(lane == slot_of(place, d, window), table, 0.0)
            ids = jnp.sum(mine, axis=1, keepdims=True).astype(jnp.int32)
            sel_ref[place * cap : (place + 1) * cap] = (ids == column).astype(f32).astype(bf16)
        if i == 0:
            grid_copy.wait()
        out_ref[part] = mm(sel_ref[part], grid_ref[...]).astype(bf16)
        copies += start_all([pltpu.make_async_copy(out_ref.at[part], out_hbm.at[part], sems.at[2 + i])])
    for copy in copies:
        copy.wait()


def gather(send_rows, grid_lat):
    window, cap = send_rows.shape[1:]
    shape = (window * cap, grid_lat.shape[1])
    return pl.pallas_call(
        gather_kernel,
        out_shape=jax.ShapeDtypeStruct(shape, bf16),
        in_specs=[HBM, HBM],
        out_specs=HBM,
        scratch_shapes=[
            pltpu.VMEM(send_rows.shape, jnp.int32),
            pltpu.VMEM(grid_lat.shape, bf16),
            pltpu.VMEM((shape[0], grid_lat.shape[0]), bf16),
            pltpu.VMEM(shape, bf16),
            pltpu.SemaphoreType.DMA((2 + shape[0] // GATHER,)),
        ],
        compiler_params=pltpu.CompilerParams(vmem_limit_bytes=VMEM),
        cost_estimate=QUICK,
        name="gather_rows",
    )(send_rows, grid_lat)


def own_kernel(
    edges_hbm, mesh_hbm, w1_hbm, out_hbm, pre_hbm,
    edges_ref, mesh_ref, w1_ref, out_ref, pre_ref, sem,
):
    width = edges_ref.shape[1]
    nodes = mesh_ref.shape[0]
    slots = edges_ref.shape[0] // nodes
    few = 16
    block = few * slots
    blocks = nodes // few
    loads = [
        pltpu.make_async_copy(
            edges_hbm.at[i * block : (i + 1) * block], edges_ref.at[i * block : (i + 1) * block], sem.at[i]
        )
        for i in range(blocks)
    ]
    loads += [
        pltpu.make_async_copy(mesh_hbm, mesh_ref, sem.at[blocks]),
        pltpu.make_async_copy(w1_hbm.at[:width], w1_ref.at[:width], sem.at[blocks + 1]),
        pltpu.make_async_copy(w1_hbm.at[2 * width :], w1_ref.at[width:], sem.at[blocks + 2]),
    ]
    start_all(loads)
    to = lax.broadcasted_iota(jnp.int32, (block, block), 0)
    at = lax.broadcasted_iota(jnp.int32, (block, block), 1)
    turn = (at == (to % few) * slots + to // few).astype(f32).astype(bf16)
    for i in range(blocks):
        loads[i].wait()
        rows = mm(turn, edges_ref[i * block : (i + 1) * block]).astype(bf16)
        for k in range(slots):
            out_ref[k * nodes + i * few : k * nodes + (i + 1) * few] = rows[k * few : (k + 1) * few]
    copies = start_all([pltpu.make_async_copy(out_ref, out_hbm, sem.at[0])])
    for copy in loads[blocks:]:
        copy.wait()
    for k in range(slots):
        part = slice(k * nodes, (k + 1) * nodes)
        both = jnp.concatenate([out_ref[part], mesh_ref[...]], axis=1)
        pre_ref[part] = mm(both, w1_ref[...])
        copies += start_all(
            [pltpu.make_async_copy(pre_ref.at[part], pre_hbm.at[part], sem.at[blocks + 3 + k])]
        )
    for copy in copies:
        copy.wait()


def own(edges, mesh_lat, w1):
    total, width = edges.shape
    sd = jax.ShapeDtypeStruct
    nodes = mesh_lat.shape[0]
    return pl.pallas_call(
        own_kernel,
        out_shape=[sd((total, width), bf16), sd((total, width), f32)],
        in_specs=[HBM] * 3,
        out_specs=[HBM] * 2,
        scratch_shapes=[
            pltpu.VMEM((total, width), bf16),
            pltpu.VMEM(mesh_lat.shape, bf16),
            pltpu.VMEM((2 * width, width), bf16),
            pltpu.VMEM((total, width), bf16),
            pltpu.VMEM((total, width), f32),
            pltpu.SemaphoreType.DMA((nodes // 16 + 3 + total // nodes,)),
        ],
        compiler_params=pltpu.CompilerParams(vmem_limit_bytes=VMEM),
        cost_estimate=QUICK,
        name="own_terms",
    )(edges, mesh_lat, w1)


def sigmoid(v):
    return 1.0 / (1.0 + jnp.exp(-v))


def row_mean(v):
    return jnp.mean(v, axis=-1, keepdims=True)


STEP = 512


def slot_places(src, window, cap):
    d = lax.axis_index("band")
    return ((d - src // cap + window // 2) & (window - 1)) * cap + (src & (cap - 1))


def middle_kernel(
    window, pre_hbm, arrived_hbm, w1_hbm, w2_hbm, mesh_hbm, cot_hbm, v1_hbm, n2_hbm,
    mask_hbm, src_hbm,
    new_hbm, gslot_hbm, gproj_hbm, g1_hbm,
    pre, arrived_ref, w1g_ref, w2_ref, mesh_ref, cot_ref, v1_ref, n2_ref, mask_ref,
    src_ref, new_ref, gslot_ref,
    proj, dsilu, hn, rm, agg, g1_ref, gproj_ref, sems,
):
    width = w2_ref.shape[0]
    nodes = mesh_ref.shape[0]
    total = pre_hbm.shape[0]
    steps = total // STEP
    per = STEP // nodes
    cap = arrived_ref.shape[0] // window
    small = [
        (w1_hbm.at[width : 2 * width], w1g_ref), (arrived_hbm, arrived_ref), (src_hbm, src_ref),
        (mask_hbm, mask_ref), (w2_hbm, w2_ref),
        (mesh_hbm, mesh_ref), (v1_hbm, v1_ref), (n2_hbm, n2_ref), (cot_hbm, cot_ref),
    ]
    small = [pltpu.make_async_copy(*pair, sems.at[i]) for i, pair in enumerate(small)]
    loads = []
    for i in range(steps):
        part = slice(i * STEP, (i + 1) * STEP)
        loads.append(pltpu.make_async_copy(pre_hbm.at[part], pre.at[part], sems.at[len(small) + i]))
    start_all(small[:2] + loads[:1] + small[2:5] + loads[1:] + small[5:])
    for copy in small[:2]:
        copy.wait()
    proj[...] = mm(arrived_ref[...], w1g_ref[...]).astype(bf16)
    for copy in small[2:5]:
        copy.wait()
    place = slot_places(src_ref[...], window, cap).astype(f32)
    both = jnp.transpose(jnp.concatenate([place, mask_ref[...].astype(f32)], axis=0))
    slots = place.shape[0]
    column = lax.broadcasted_iota(jnp.int32, (nodes, proj.shape[0]), 1)
    agg[...] = jnp.zeros_like(agg)
    for i in range(steps):
        part = slice(i * STEP, (i + 1) * STEP)
        hot = jnp.concatenate(
            [
                (both[:, k : k + 1].astype(jnp.int32) == column).astype(f32).astype(bf16)
                for k in range(i * per, (i + 1) * per)
            ],
            axis=0,
        )
        got = mm(hot, proj[...])
        loads[i].wait()
        v = pre[part] + got
        sig = sigmoid(v)
        hid = v * sig
        dsilu[part] = sig + hid * (1.0 - sig)
        p2 = mm(hid.astype(bf16), w2_ref[...])
        c = p2 - row_mean(p2)
        r = lax.rsqrt(row_mean(c * c) + eps)
        h = c * r
        hn[part] = h
        m = jnp.concatenate(
            [both[:, slots + k : slots + k + 1] for k in range(i * per, (i + 1) * per)], axis=0
        )
        rm[part] = r * m
        msg = h * m
        add = msg[:nodes]
        for n in range(1, per):
            add = add + msg[n * nodes : (n + 1) * nodes]
        agg[...] += add
    for copy in small[5:]:
        copy.wait()
    mesh = mesh_ref[...]
    p3 = mm(mesh, v1_ref[:width]) + mm(agg[...].astype(bf16), v1_ref[width:])
    sig = sigmoid(p3)
    a3 = p3 * sig
    p4 = mm(a3.astype(bf16), n2_ref[...])
    c = p4 - row_mean(p4)
    r = lax.rsqrt(row_mean(c * c) + eps)
    h = c * r
    new_ref[...] = (mesh.astype(f32) + h).astype(bf16)
    stores = start_all([pltpu.make_async_copy(new_ref, new_hbm, sems.at[0])])
    cot = cot_ref[...].astype(f32)
    g4 = (r * (cot - row_mean(cot) - h * row_mean(cot * h))).astype(bf16)
    g3 = (mm_t(g4, n2_ref[...]) * (sig + a3 * (1.0 - sig))).astype(bf16)
    ga = mm_t(g3, v1_ref[width:])
    agg[...] = ga - row_mean(ga)
    wide = 2 * STEP
    for i in range(total // wide):
        part = slice(i * wide, (i + 1) * wide)
        ga = jnp.concatenate([agg[...]] * (wide // nodes), axis=0)
        h = hn[part]
        g2 = rm[part] * (ga - h * row_mean(ga * h))
        g1_ref[part] = (mm_t(g2.astype(bf16), w2_ref[...]) * dsilu[part]).astype(bf16)
    stores += start_all([pltpu.make_async_copy(g1_ref, g1_hbm, sems.at[1])])
    src = slot_places(src_ref[...], window, cap)
    rows = 512
    for i in range(gproj_ref.shape[0] // rows):
        part = slice(i * rows, (i + 1) * rows)
        slot = lax.broadcasted_iota(jnp.int32, (rows, nodes), 0) + i * rows
        sel = jnp.concatenate(
            [(slot == src[k : k + 1]).astype(f32).astype(bf16) for k in range(slots)], axis=1
        )
        gp = mm(sel, g1_ref[...]).astype(bf16)
        gproj_ref[part] = gp
        gslot_ref[part] = mm_t(gp, w1g_ref[...]).astype(bf16)
        stores += start_all(
            [
                pltpu.make_async_copy(gslot_ref.at[part], gslot_hbm.at[part], sems.at[2 + i]),
                pltpu.make_async_copy(gproj_ref.at[part], gproj_hbm.at[part], sems.at[6 + i]),
            ]
        )
    for copy in stores:
        copy.wait()


SHARE = [4 * kz + 2 * ky for ky in range(2) for kz in (2, 3, 0, 1)]
PIECES = 4


def middle(window, pre, arrived, w1, w2, mesh_lat, cot, v1, n2, mask, src):
    total, width = pre.shape
    nodes = mesh_lat.shape[0]
    sd = jax.ShapeDtypeStruct
    vm = pltpu.VMEM
    return pl.pallas_call(
        functools.partial(middle_kernel, window),
        out_shape=[
            sd((nodes, width), bf16), sd(arrived.shape, bf16), sd(arrived.shape, bf16),
            sd((total, width), bf16),
        ],
        in_specs=[HBM] * 10,
        out_specs=[HBM] * 4,
        scratch_shapes=[
            vm((total, width), f32),
            vm(arrived.shape, bf16),
            vm(w2.shape, bf16),
            vm(w2.shape, bf16),
            vm(mesh_lat.shape, bf16),
            vm(cot.shape, bf16),
            vm(v1.shape, bf16),
            vm(n2.shape, bf16),
            vm(mask.shape, jnp.int32),
            vm(src.shape, jnp.int32),
            vm(mesh_lat.shape, bf16),
            vm(arrived.shape, bf16),
            vm(arrived.shape, bf16),
            vm((total, width), f32),
            vm((total, width), f32),
            vm((total, 1), f32),
            vm((nodes, width), f32),
            vm((total, width), bf16),
            vm(arrived.shape, bf16),
            pltpu.SemaphoreType.DMA((10 + total // STEP,)),
        ],
        compiler_params=pltpu.CompilerParams(vmem_limit_bytes=VMEM),
        cost_estimate=QUICK,
        name="edges_and_nodes",
    )(pre, arrived, w1, w2, mesh_lat, cot, v1, n2, mask, src)


def terms_kernel(edges_ref, g1_ref, mesh_ref, arrived_ref, gproj_ref, *rest):
    keep, send, term = rest[:PIECES], rest[PIECES:-1], rest[-1]
    width = g1_ref.shape[1]
    nodes = mesh_ref.shape[0]
    g1 = g1_ref[...]
    term[:width] = outer_sum(edges_ref[...], g1)
    term[width : 2 * width] = outer_sum(arrived_ref[...], gproj_ref[...])
    gsum = g1[:nodes].astype(f32)
    for k in range(1, g1.shape[0] // nodes):
        gsum = gsum + g1[k * nodes : (k + 1) * nodes].astype(f32)
    term[2 * width :] = outer_sum(mesh_ref[...], gsum.astype(bf16))
    share = keep[0].shape[1]
    d = lax.axis_index("band")
    for i, k in enumerate(SHARE):
        at = pl.ds(pl.multiple_of((d ^ k ^ 1) * share, share), share)
        send[i // 2][i % 2] = term[at].astype(bf16)
    for i, k in enumerate(SHARE):
        at = pl.ds(pl.multiple_of((d ^ k) * share, share), share)
        keep[i // 2][i % 2] = term[at]


def terms(edges, g1, mesh_lat, arrived, gproj):
    width = g1.shape[1]
    share = (2, 3 * width // 16, width)
    sd = jax.ShapeDtypeStruct
    out = pl.pallas_call(
        terms_kernel,
        out_shape=[sd(share, f32)] * PIECES + [sd(share, bf16)] * PIECES,
        in_specs=[VM] * 5,
        out_specs=[VM] * (2 * PIECES),
        scratch_shapes=[pltpu.VMEM((3 * width, width), f32)],
        compiler_params=pltpu.CompilerParams(vmem_limit_bytes=16 << 20),
        cost_estimate=QUICK,
        name="w1_terms",
    )(edges, g1, mesh_lat, arrived, gproj)
    return out[:PIECES], out[PIECES:]


def share_sum(keep, send):
    full = [mine + swap(other, 1).astype(f32) for mine, other in zip(keep, send)]
    half = len(full) // 2
    full = [mine + swap(other.astype(bf16), 2).astype(f32) for mine, other in zip(full, full[half:])]
    far, near = full
    others = [swap(far[0].astype(bf16), 8), swap(far[1].astype(bf16), 12), swap(near[1].astype(bf16), 4)]
    return near[0], others


def grid_kernel(ids_ref, rows_ref, out_hbm, at_ref, out_ref, sems):
    window, cap = ids_ref.shape[1:]
    d = lax.axis_index("band")
    for place in range(window):
        at_ref[:, place * cap : (place + 1) * cap] = ids_ref[0, pl.ds(slot_of(place, d, window), 1), :]
    ids = at_ref[...]
    block = 512
    copies = []
    for i in range(out_ref.shape[0] // block):
        part = slice(i * block, (i + 1) * block)
        row = lax.broadcasted_iota(jnp.int32, (block, ids.shape[1]), 0) + i * block
        sel = (row == ids).astype(f32).astype(bf16)
        out_ref[part] = mm(sel, rows_ref[...]).astype(bf16)
        copies += start_all([pltpu.make_async_copy(out_ref.at[part], out_hbm.at[part], sems.at[i])])
    for copy in copies:
        copy.wait()


def grid_sum(send_rows, rows, grid_rows):
    slots, width = rows.shape
    return pl.pallas_call(
        grid_kernel,
        out_shape=jax.ShapeDtypeStruct((grid_rows, width), bf16),
        in_specs=[VM] * 2,
        out_specs=HBM,
        scratch_shapes=[
            pltpu.VMEM((1, slots), jnp.int32),
            pltpu.VMEM((grid_rows, width), bf16),
            pltpu.SemaphoreType.DMA((grid_rows // 256,)),
        ],
        compiler_params=pltpu.CompilerParams(vmem_limit_bytes=10 << 20),
        cost_estimate=pl.CostEstimate(
            flops=2 * grid_rows * slots * width, bytes_accessed=4 << 20, transcendentals=0
        ),
        name="grid_sum",
    )(send_rows, rows)


def per_device_all(
    grid_lat, mesh_lat, edge_lat, edge_w1, edge_w2, node_w1, node_w2, mesh_cot,
    send_rows, edge_src, edge_mask,
):
    width = mesh_lat.shape[1]
    nodes, slots = edge_src.shape
    arrived = exchange(gather(send_rows, grid_lat))

    edges, pre = own(edge_lat.reshape(nodes * slots, width), mesh_lat, edge_w1)
    src = jnp.transpose(edge_src)
    mask = jnp.transpose(edge_mask)

    mesh_new, gslot, gproj, g1 = middle(
        send_rows.shape[1], pre, arrived, edge_w1, edge_w2, mesh_lat, mesh_cot, node_w1,
        node_w2, mask, src,
    )
    returned = exchange(gslot)
    keep, send = terms(edges, g1, mesh_lat, arrived, gproj)
    mine, others = share_sum(keep, send)
    grid_grad = grid_sum(send_rows, returned, grid_lat.shape[0])
    grid_grad, w1_grad = lax.optimization_barrier((grid_grad, mine))
    for other in others:
        w1_grad = w1_grad + other.astype(f32)
    return (mesh_new, grid_grad, w1_grad)


def solution(mesh):
    in_specs = (
        P(("group", "band"), None),
        P(("group", "band"), None),
        P(("group", "band"), None, None),
        P(),
        P(),
        P(),
        P(),
        P(("group", "band"), None),
        P("band", None, None),
        P("band", None),
        P("band", None),
    )
    out_specs = (P(("group", "band"), None), P(("group", "band"), None), P(("group", "band"), None))

    def step(*args):
        window = args[8].shape[1]
        every = mesh.shape["band"] == window == 16
        body = per_device_all if every else per_device_window
        return jax.shard_map(
            body, mesh=mesh, in_specs=in_specs, out_specs=out_specs, check_vma=False
        )(*args)

    return step
```
